512 devices in a mesh: inst: 16 (over y, core), tp: 32 (over z, x).
Axes of the slice: x: 4, y: 8, z: 8, core: 2. Of those that a mesh axis runs over, the one named last changes fastest.
Arguments:
- queries: bfloat16 [256, 8192], P('inst', 'tp'), may hold values from -5 to 5
- home_kv: bfloat16 [384, 32, 128, 256], P('inst', 'tp'), may hold values from -5 to 5, as said below
- lent_kv: bfloat16 [256, 32, 128, 256], P('inst', 'tp'), may hold values from -5 to 5, as said below
- page_table: int32 [256, 2], P('inst'), may hold values from -1 to 23, as said below
- borrowed: int32 [256, 2], P('inst'), may hold values from -1 to 255, as said below
- lengths: int32 [256], P('inst'), may hold values from 1 to 512, as said below
- out_weight: bfloat16 [8192, 4096], P('tp'), may hold values from -0.25 to 0.25
Outputs:
- projected: bfloat16 [256, 4096], P('inst', 'tp')
The draws below stay inside these ranges and needn't reach their ends.
Inputs may be any that keep to these rules, and one draw needn't show every extreme that they name: `page_table`: row r lists the home pages of request r in sequence order by their number within its instance's 24 pages, then -1 where it has fewer than 2; every request has one or more, and each page of an instance is listed exactly once. `borrowed`: row r lists the pages that request r holds after its home pages, in sequence order, as the lending instance times 16 plus the slot, then -1; each of the 256 lent slots is listed exactly once, and a slot may lie in the request's own instance. `lengths`: with p the number of entries of the request in page_table and borrowed other than -1, the length is above 128 * (p - 1) and at most 128 * p. `home_kv`: the copies of one key-value head along dimension 1 are equal. `lent_kv`: the copies of one key-value head along dimension 1 are equal.
All inputs are finite; a program needn't handle non-finite values.
Results may differ from the reference program's by a relative error of at most 0.0085.
Values may be sent and summed in bfloat16 or wider, within the bound.
A program may use at most 64 MiB of HBM per device.

```python
import math
import jax
import jax.numpy as jnp
from jax import lax

QH = 64
KVH = 8
HD = 128
D_OUT = 4096
PAGE = 128
HOME_MOST = 2
BORROW_MOST = 2
REQ_INST = 16
REQS = 256
QH_DEV = 2
COPIES = 32
HOME_POOL = 24
LENT_POOL = 16
N_INST = 16


def shuffle_requests(inst_key):
    return jax.random.permutation(inst_key, REQ_INST)


def shuffle_pool(inst_key):
    return jax.random.permutation(inst_key, HOME_POOL)


def page_layout(key):
    layout_key = jax.random.fold_in(key, 977)
    home_key, borrow_key, slot_key, pool_key, fill_key = jax.random.split(layout_key, 5)
    ranking = jax.vmap(shuffle_requests)(jax.random.split(home_key, N_INST))
    home_count = 1 + (ranking < REQ_INST // 2).astype(jnp.int32)
    home_start = jnp.cumsum(home_count, axis=1) - home_count
    pool_order = jax.vmap(shuffle_pool)(jax.random.split(pool_key, N_INST))
    page_index = jnp.arange(HOME_MOST, dtype=jnp.int32)
    pick_index = jnp.minimum(home_start[..., None] + page_index, HOME_POOL - 1)
    home_table = jnp.take_along_axis(pool_order, pick_index.reshape(N_INST, REQ_INST * HOME_MOST), axis=1)
    home_table = home_table.reshape(N_INST, REQ_INST, HOME_MOST)
    home_table = jnp.where(page_index < home_count[..., None], home_table, -1).reshape(REQS, HOME_MOST)
    longest = jnp.argmin(ranking[0]).astype(jnp.int32)
    shortest = jnp.argmax(ranking[0]).astype(jnp.int32)
    base_rank = jax.random.permutation(borrow_key, REQS).astype(jnp.int32)
    first_pos = jnp.argmin(base_rank).astype(jnp.int32)
    global_rank = base_rank.at[first_pos].set(base_rank[longest]).at[longest].set(0)
    last_pos = jnp.argmax(global_rank).astype(jnp.int32)
    global_rank = global_rank.at[last_pos].set(global_rank[shortest]).at[shortest].set(REQS - 1)
    borrow_count = jnp.where(global_rank < REQS // 4, 2, jnp.where(global_rank < 3 * REQS // 4, 1, 0)).astype(jnp.int32)
    borrow_start = jnp.cumsum(borrow_count) - borrow_count
    slot_order = jax.random.permutation(slot_key, REQS)
    borrow_index = jnp.arange(BORROW_MOST, dtype=jnp.int32)
    chosen = slot_order[jnp.minimum(borrow_start[:, None] + borrow_index, REQS - 1)]
    borrow_table = jnp.where(borrow_index < borrow_count[:, None], chosen, -1).astype(jnp.int32)
    last_fill = jax.random.randint(fill_key, (REQS,), 1, PAGE + 1).astype(jnp.int32)
    last_fill = last_fill.at[longest].set(PAGE).at[shortest].set(1)
    context = ((home_count.reshape(REQS) + borrow_count - 1) * PAGE + last_fill).astype(jnp.int32)
    return (home_table.astype(jnp.int32), borrow_table, context)


def spread_heads(values_drawn):
    return jnp.repeat(values_drawn, COPIES // KVH, axis=1)


def draw_page_table(key, part):
    return page_layout(key)[0]


def draw_borrowed(key, part):
    return page_layout(key)[1]


def draw_lengths(key, part):
    return page_layout(key)[2]


def draw_queries(key, part):
    key = jax.random.fold_in(key, 11)
    values_drawn = jnp.clip(jax.random.normal(key, (REQS, QH, HD), jnp.float32), -5.0, 5.0)
    return values_drawn.reshape(REQS, QH * HD).astype(jnp.bfloat16)


def draw_home_kv(key, part):
    key = jax.random.fold_in(key, 23)
    pool_shape = (N_INST * HOME_POOL, KVH, PAGE, 2 * HD)
    values_drawn = jnp.clip(jax.random.normal(key, pool_shape, jnp.float32), -5.0, 5.0)
    return spread_heads(values_drawn).astype(jnp.bfloat16)


def draw_lent_kv(key, part):
    key = jax.random.fold_in(key, 37)
    pool_shape = (N_INST * LENT_POOL, KVH, PAGE, 2 * HD)
    values_drawn = jnp.clip(jax.random.normal(key, pool_shape, jnp.float32), -5.0, 5.0)
    return spread_heads(values_drawn).astype(jnp.bfloat16)


def level_of(own_key, extent, pieces, smallest, top_value):
    level = 1.0
    for position, blocks in pieces:
        steps = jax.random.uniform(jax.random.fold_in(jax.random.fold_in(own_key, 6), position), (blocks,), jnp.float32, smallest / len(pieces), top_value / len(pieces))
        level = level * jnp.repeat(jnp.exp(steps), extent[position] // blocks).reshape((-1,) + (1,) * (len(extent) - 1 - position))
    return level


def normal_values(key, shape, scale, most, pieces=(), held_as=jnp.bfloat16):
    loudness = level_of(key, shape, pieces, -0.22, 0.18) if pieces else 1.0
    result = jax.random.normal(key, shape, jnp.float32) * scale * loudness
    return jnp.minimum(jnp.maximum(result, -most), most).astype(held_as)


def setup_inputs(seed: int = 0) -> dict:
    key_list = jax.random.split(jax.random.key(seed), 8)
    return {
        "queries": draw_queries(jax.random.fold_in(key_list[7], 71), 0),
        "home_kv": draw_home_kv(jax.random.fold_in(key_list[7], 71), 0),
        "lent_kv": draw_lent_kv(jax.random.fold_in(key_list[7], 71), 0),
        "page_table": draw_page_table(jax.random.fold_in(key_list[7], 71), 0),
        "borrowed": draw_borrowed(jax.random.fold_in(key_list[7], 71), 0),
        "lengths": draw_lengths(jax.random.fold_in(key_list[7], 71), 0),
        "out_weight": normal_values(key_list[6], (QH * HD, D_OUT), (QH * HD // 16) ** -0.5, 0.25, ((0, 32),)),
    }


sentinel = -1e+30

def page_stats(scores, usable):
    masked = jnp.where(usable, scores, sentinel)
    maxima = lax.optimization_barrier(jnp.max(masked, axis=-1))
    weights = jnp.where(usable, jnp.exp(masked - maxima[..., None]), 0.0)
    rounded = weights.astype(jnp.bfloat16)
    totals = lax.optimization_barrier(jnp.sum(rounded.astype(jnp.float32), axis=-1))
    return (maxima, totals, rounded)

def reference(queries, home_kv, lent_kv, page_table, borrowed, lengths, out_weight):
    groups = N_INST + 1
    score_scale = 1.0 / math.sqrt(HD)

    def attend(request):
        instance = request // REQ_INST
        table_row = page_table[request]
        borrow_row = borrowed[request]
        length = lengths[request]
        home_count = jnp.sum((table_row >= 0).astype(jnp.int32))
        home_index = (instance * HOME_POOL + jnp.maximum(table_row, 0)).astype(jnp.int32)
        lent_index = jnp.maximum(borrow_row, 0).astype(jnp.int32)
        page_rows = jnp.concatenate([home_kv[home_index], lent_kv[lent_index]], axis=0)
        slot_order = jnp.arange(HOME_MOST + BORROW_MOST, dtype=jnp.int32)
        first_token = jnp.where(slot_order < HOME_MOST, slot_order, home_count + slot_order - HOME_MOST) * PAGE
        present = jnp.concatenate([table_row >= 0, borrow_row >= 0])
        group_of = jnp.concatenate([jnp.full((HOME_MOST,), N_INST, jnp.int32), (borrow_row // LENT_POOL).astype(jnp.int32)])
        tokens = first_token[:, None] + jnp.arange(PAGE, dtype=jnp.int32)[None, :]
        usable = present[:, None] & (tokens < length)
        query_heads = queries[request].astype(jnp.float32).reshape(COPIES, QH_DEV, HD)
        key_part = page_rows[..., :HD].astype(jnp.float32)
        value_part = page_rows[..., HD:].astype(jnp.float32)
        scores = jnp.einsum('cgd,pctd->pcgt', query_heads, key_part, precision=lax.Precision.HIGHEST) * score_scale
        maxima, totals, rounded = page_stats(scores, usable[:, None, None, :])
        partial_out = jnp.einsum('pcgt,pctd->pcgd', rounded.astype(jnp.float32), value_part, precision=lax.Precision.HIGHEST)
        member = group_of[None, :] == jnp.arange(groups, dtype=jnp.int32)[:, None]
        member_grid = member[:, :, None, None]
        group_peak = lax.optimization_barrier(jnp.max(jnp.where(member_grid, maxima[None], sentinel), axis=1))
        factor = jnp.where(member_grid, jnp.exp(jnp.where(member_grid, maxima[None] - group_peak[:, None], sentinel)), 0.0)
        weight_sum = lax.optimization_barrier(jnp.sum(factor * totals[None], axis=1))
        out_sum = lax.optimization_barrier(jnp.sum(factor[..., None] * partial_out[None], axis=1))
        floor_sum = jnp.maximum(weight_sum, 1.0)
        group_out = lax.optimization_barrier((out_sum / floor_sum[..., None]).astype(jnp.bfloat16)).astype(jnp.float32)
        group_lse = group_peak + jnp.log(floor_sum)
        summit = lax.optimization_barrier(jnp.max(group_lse, axis=0))
        shares = jnp.exp(group_lse - summit[None])
        merged = lax.optimization_barrier(jnp.sum(shares[..., None] * group_out, axis=0)) / lax.optimization_barrier(jnp.sum(shares, axis=0))[..., None]
        return merged.astype(jnp.bfloat16).reshape(QH * HD)
    attended = lax.map(attend, jnp.arange(REQS, dtype=jnp.int32))
    return jnp.dot(attended, out_weight, preferred_element_type=jnp.float32).astype(jnp.bfloat16)
```

```python
import functools
import math

import jax
import jax.numpy as jnp
from jax import lax
from jax.experimental import pallas as pl
from jax.experimental.pallas import tpu as pltpu
from jax.sharding import PartitionSpec as P

HD = 128
PAGE = 128
RANKS = 2
SENTINEL = -1e30
F32 = jnp.float32
BF16 = jnp.bfloat16
I32 = jnp.int32


def column(values, shape):
    row = lax.broadcasted_iota(I32, shape, 0)
    out = jnp.full(shape, values[0], I32)
    for r in range(1, len(values)):
        out = jnp.where(row == r, values[r], out)
    return out


def dot(a, b, dims=((1,), (0,))):
    return lax.dot_general(a, b, (dims, ((), ())), preferred_element_type=F32)


def by_head(x):
    return jnp.concatenate([x[:, :HD], x[:, HD:]], axis=0)


def by_lane(x):
    rows = x.shape[0] // 2
    return jnp.concatenate([x[:rows], x[rows:]], axis=1)


def fused(
    n_inst, nz, nx,
    q_hbm, home_hbm, lent_hbm, table_hbm, borrowed_hbm, lengths_hbm, weight_hbm,
    out_ref,
    q_v, home_v, lent_v, weight_v, table_s, borrowed_s, lengths_s,
    ask_out, ask_in, count_out, count_in, part_out, part_in, stat_out, stat_in, proj_out, proj_in,
    load_sem, send_sem, recv_sem,
):
    n_tp = nz * nx
    slots = lent_v.shape[0]
    reqs = q_v.shape[0]
    me = lax.axis_index("inst")
    tp = lax.axis_index("tp")
    my_z, my_x = tp // nx, tp % nx
    scale = 1.0 / math.sqrt(HD)

    loads = []
    for i, (src, dst) in enumerate(
        [
            (table_hbm, table_s),
            (borrowed_hbm, borrowed_s),
            (lengths_hbm, lengths_s),
            (q_hbm, q_v),
            (home_hbm, home_v),
            (lent_hbm, lent_v),
            (weight_hbm, weight_v),
        ]
    ):
        copy = pltpu.make_async_copy(src, dst, load_sem.at[i])
        copy.start()
        loads.append(copy)

    barrier = pltpu.get_barrier_semaphore()
    for k in range(1, n_inst):
        pl.semaphore_signal(barrier, 1, device_id={"inst": (me + k) % n_inst})
    for k in range(1, n_tp):
        pl.semaphore_signal(barrier, 1, device_id={"tp": (tp + k) % n_tp})

    for copy in loads[:4]:
        copy.wait()

    table = [[table_s[r, j] for j in range(RANKS)] for r in range(reqs)]
    length = [lengths_s[r] for r in range(reqs)]
    beyond = [
        length[r] - PAGE * sum((t >= 0).astype(I32) for t in table[r]) for r in range(reqs)
    ]
    shape = (reqs, 128)
    borrow = [column([borrowed_s[r, j] for r in range(reqs)], shape) for j in range(RANKS)]
    left = column(beyond, shape)
    counted = [jnp.clip(left - PAGE * j, 0, PAGE).astype(F32) for j in range(RANKS)]
    lane = lax.broadcasted_iota(I32, shape, 1)
    total_slots = n_inst * slots
    wanted, counts = [], []
    for base in range(0, total_slots, 128):
        hit = [b == lane + base for b in borrow]
        wanted.append((hit[0] | hit[1]).astype(F32))
        both = jnp.where(hit[0], counted[0], 0.0) + jnp.where(hit[1], counted[1], 0.0)
        counts.append(jnp.sum(both, axis=0, keepdims=True))
    wanted = jnp.concatenate(wanted, axis=1)[:, :total_slots].astype(BF16)
    counts = jnp.concatenate(counts, axis=1)
    q = q_v[...]
    asked = dot(wanted, q, ((0,), (0,))).astype(BF16)
    ask_out[...] = asked.reshape(n_inst, slots, 2 * HD)
    count_out[...] = counts
    ask_in[n_inst - 1] = ask_out[me]
    count_in[n_inst - 1] = counts

    pl.semaphore_wait(barrier, n_inst + n_tp - 2)

    def send(src, dst, phase, to):
        pltpu.make_async_remote_copy(
            src_ref=src, dst_ref=dst, send_sem=send_sem.at[phase], recv_sem=recv_sem.at[phase], device_id=to
        ).start()

    def arrive(ref, count, phase):
        part = ref.at[pl.ds(0, count)]
        pltpu.make_async_copy(part, part, recv_sem.at[phase]).wait()

    def sent(ref, count, phase):
        part = ref.at[pl.ds(0, count)]
        pltpu.make_async_copy(part, part, send_sem.at[phase]).wait()

    order = sorted(range(1, n_inst), key=lambda k: -min(k, n_inst - k))
    for k in order:
        to = (me + k) % n_inst
        send(ask_out.at[to], ask_in.at[k - 1], 0, {"inst": to})
        send(count_out, count_in.at[k - 1], 1, {"inst": to})

    row = lax.broadcasted_iota(I32, (2 * reqs, PAGE), 0) % reqs
    token = lax.broadcasted_iota(I32, (2 * reqs, PAGE), 1)
    q2 = by_head(q)
    loads[4].wait()
    scores = [jnp.zeros((2 * reqs, PAGE), F32) for _ in range(RANKS)]
    usable = [jnp.zeros((2 * reqs, PAGE), I32) for _ in range(RANKS)]
    for r in range(reqs):
        for j in range(RANKS):
            page = jnp.maximum(table[r][j], 0)
            s = dot(q2, home_v[page, 0, :, :HD], ((1,), (1,)))
            scores[j] = jnp.where(row == r, s, scores[j])
            here = jnp.where(table[r][j] >= 0, length[r] - PAGE * j, 0)
            usable[j] = jnp.where(row == r, here, usable[j])
    usable = [token < u for u in usable]
    scores = [jnp.where(u, s * scale, SENTINEL) for u, s in zip(usable, scores)]
    home_max = jnp.max(jnp.maximum(scores[0], scores[1]), axis=1, keepdims=True)
    home_w = [
        jnp.where(u, jnp.exp(s - home_max), 0.0).astype(BF16) for u, s in zip(usable, scores)
    ]
    home_total = sum(jnp.sum(w.astype(F32), axis=1, keepdims=True) for w in home_w)
    home_sum = jnp.zeros((2 * reqs, HD), F32)
    for r in range(reqs):
        o = 0.0
        for j in range(RANKS):
            page = jnp.maximum(table[r][j], 0)
            o = o + dot(home_w[j], home_v[page, 0, :, HD:])
        home_sum = jnp.where(row == r, o, home_sum)

    loads[5].wait()
    arrive(ask_in, n_inst - 1, 0)
    arrive(count_in, n_inst - 1, 1)
    q_lent = ask_in[0]
    for k in range(1, n_inst):
        q_lent = q_lent + ask_in[k]
    q_lent = by_head(q_lent)
    count_row = jnp.sum(count_in[...], axis=0)
    wide = (slots, count_row.shape[1])
    mine = lax.broadcasted_iota(I32, wide, 1) == me * slots + lax.broadcasted_iota(I32, wide, 0)
    count_col = jnp.sum(jnp.where(mine, count_row, 0.0), axis=1, keepdims=True)
    count_col = jnp.concatenate([count_col, count_col], axis=0)
    lrow = lax.broadcasted_iota(I32, (2 * slots, PAGE), 0)
    lslot = lrow % slots
    llane = lax.broadcasted_iota(I32, (2 * slots, PAGE), 1)
    s = jnp.zeros((2 * slots, PAGE), F32)
    for p in range(slots):
        s = jnp.where(lslot == p, dot(q_lent, lent_v[p, 0, :, :HD], ((1,), (1,))), s)
    ok = llane < count_col.astype(I32)
    s = jnp.where(ok, s * scale, SENTINEL)
    lent_max = jnp.max(s, axis=1, keepdims=True)
    w = jnp.where(ok, jnp.exp(s - lent_max), 0.0).astype(BF16)
    lent_total = jnp.sum(w.astype(F32), axis=1, keepdims=True)
    o = jnp.zeros((2 * slots, HD), F32)
    for p in range(slots):
        o = jnp.where(lslot == p, dot(w, lent_v[p, 0, :, HD:]), o)
    part = by_lane(o).astype(BF16)
    stats = jnp.where(llane == lrow, lent_max, 0.0) + jnp.where(
        llane == lrow + 2 * slots, lent_total, 0.0
    )
    stats = jnp.sum(stats, axis=0, keepdims=True)
    part_out[...] = part
    stat_out[...] = stats
    part_in[n_inst - 1] = part
    stat_in[n_inst - 1] = stats
    for k in order:
        to = (me + k) % n_inst
        send(stat_out, stat_in.at[k - 1], 3, {"inst": to})
        send(part_out, part_in.at[k - 1], 2, {"inst": to})

    two = jnp.concatenate(borrow, axis=0)
    gather = []
    for base in range(0, total_slots, 128):
        i = base + lax.broadcasted_iota(I32, two.shape, 1)
        name = (me - i // slots - 1) % n_inst * slots + i % slots
        gather.append((two == name).astype(F32))
    gather = jnp.concatenate(gather, axis=1)[:, :total_slots].astype(BF16)
    lane2 = lax.broadcasted_iota(I32, two.shape, 1)
    lender = ((me - lane2 - 1) % n_inst == two // slots) & (lane2 < n_inst) & (two >= 0)
    lender = lender[:, :n_inst].astype(F32).astype(BF16)
    slot = jnp.where(two >= 0, two % slots, -1)

    arrive(stat_in, n_inst - 1, 3)
    left_over = stat_in[...].reshape(n_inst, 128)
    found = jnp.zeros(two.shape, F32)
    for _ in range(3):
        piece = left_over.astype(BF16)
        found = found + dot(lender, piece)
        left_over = left_over - piece.astype(F32)
    present = two[:, :1] >= 0

    def pick(kind, absent):
        value = jnp.sum(jnp.where(lane2 == slot + kind * slots, found, 0.0), axis=1, keepdims=True)
        value = jnp.where((slot[:, :1] >= 0), value, absent)
        return [value[j * reqs : (j + 1) * reqs] for j in range(RANKS)]

    max0, max1 = pick(0, SENTINEL), pick(1, SENTINEL)
    tot0, tot1 = pick(2, 0.0), pick(3, 0.0)
    page_max = [jnp.concatenate([max0[j], max1[j]], axis=0) for j in range(RANKS)]
    page_total = [jnp.concatenate([tot0[j], tot1[j]], axis=0) for j in range(RANKS)]
    summit = jnp.maximum(home_max, jnp.maximum(page_max[0], page_max[1]))
    home_share = jnp.exp(home_max - summit)
    share = [jnp.exp(m - summit) for m in page_max]
    total = home_share * home_total + share[0] * page_total[0] + share[1] * page_total[1]
    total = jnp.maximum(total, 1.0)
    arrive(part_in, n_inst - 1, 2)
    got = dot(gather, part_in[...].reshape(total_slots, 2 * HD))
    attended = home_share * home_sum
    for j in range(RANKS):
        attended = attended + share[j] * by_head(got[j * reqs : (j + 1) * reqs])
    attended = by_lane(attended / total).astype(BF16)

    loads[6].wait()
    steps = sorted(range(nz), key=lambda d: -min(d, nz - d))
    for n, dz in enumerate(steps):
        z = (my_z + dz) % nz
        start = pl.multiple_of(z * (nx * 128), nx * 128)
        block = dot(attended, weight_v[:, pl.ds(start, nx * 128)]).astype(BF16)
        for x in range(nx):
            proj_out[n * nx + x] = block[:, x * 128 : (x + 1) * 128]
        for x in range(nx):
            place = n * nx + (x - my_x) % nx
            to = {"tp": z * nx + x}
            if dz == 0:

                @pl.when(x != my_x)
                def _():
                    send(proj_out.at[n * nx + x], proj_in.at[place - 1], 4, to)
            else:
                send(proj_out.at[n * nx + x], proj_in.at[place], 4, to)
    result = proj_out[(nz - 1) * nx + my_x].astype(F32)
    arrive(proj_in, n_tp - 1, 4)
    result = result + jnp.sum(proj_in[...].astype(F32), axis=0)
    out_ref[...] = result.astype(out_ref.dtype)

    sent(ask_in, n_inst - 1, 0)
    sent(count_in, n_inst - 1, 1)
    sent(part_in, n_inst - 1, 2)
    sent(stat_in, n_inst - 1, 3)
    sent(proj_in, n_tp - 1, 4)


def shards(nx, queries, home_kv, lent_kv, page_table, borrowed, lengths, out_weight):
    n_inst, n_tp = lax.axis_size("inst"), lax.axis_size("tp")
    reqs = queries.shape[0]
    slots = lent_kv.shape[0]
    cols = out_weight.shape[1] // n_tp
    lanes = -(-n_inst * slots // 128) * 128
    return pl.pallas_call(
        functools.partial(fused, n_inst, n_tp // nx, nx),
        out_shape=jax.ShapeDtypeStruct((reqs, cols), BF16),
        in_specs=[pl.BlockSpec(memory_space=pl.ANY)] * 7,
        out_specs=pl.BlockSpec(memory_space=pltpu.VMEM),
        scratch_shapes=[
            pltpu.VMEM(queries.shape, BF16),
            pltpu.VMEM(home_kv.shape, BF16),
            pltpu.VMEM(lent_kv.shape, BF16),
            pltpu.VMEM(out_weight.shape, BF16),
            pltpu.SMEM(page_table.shape, I32),
            pltpu.SMEM(borrowed.shape, I32),
            pltpu.SMEM(lengths.shape, I32),
            pltpu.VMEM((n_inst, slots, 2 * HD), BF16),
            pltpu.VMEM((n_inst, slots, 2 * HD), BF16),
            pltpu.VMEM((1, lanes), F32),
            pltpu.VMEM((n_inst, 1, lanes), F32),
            pltpu.VMEM((slots, 2 * HD), BF16),
            pltpu.VMEM((n_inst, slots, 2 * HD), BF16),
            pltpu.VMEM((1, 128), F32),
            pltpu.VMEM((n_inst, 1, 128), F32),
            pltpu.VMEM((n_tp, reqs, cols), BF16),
            pltpu.VMEM((n_tp - 1, reqs, cols), BF16),
            pltpu.SemaphoreType.DMA((7,)),
            pltpu.SemaphoreType.DMA((5,)),
            pltpu.SemaphoreType.DMA((5,)),
        ],
        compiler_params=pltpu.CompilerParams(
            collective_id=0, has_side_effects=True, vmem_limit_bytes=40 * 1024 * 1024
        ),
    )(queries, home_kv, lent_kv, page_table, borrowed, lengths, out_weight)


def solution(mesh):
    n_tp = mesh.shape["tp"]
    nx = 4 if n_tp % 4 == 0 else 1
    placed = (
        P("inst", "tp"),
        P("inst", "tp", None, None),
        P("inst", "tp", None, None),
        P("inst", None),
        P("inst", None),
        P("inst"),
        P("tp", None),
    )
    return jax.shard_map(
        functools.partial(shards, nx), mesh=mesh, in_specs=placed, out_specs=P("inst", "tp"), check_vma=False
    )
```

```python
import functools
import math

import jax
import jax.numpy as jnp
from jax import lax
from jax.experimental import pallas as pl
from jax.experimental.pallas import tpu as pltpu
from jax.sharding import PartitionSpec as P

HD = 128
PAGE = 128
RANKS = 2
SENTINEL = -1e30
F32 = jnp.float32
BF16 = jnp.bfloat16
I32 = jnp.int32


def column(values, shape):
    row = lax.broadcasted_iota(I32, shape, 0)
    out = jnp.full(shape, values[0], I32)
    for r in range(1, len(values)):
        out = jnp.where(row == r, values[r], out)
    return out


def dot(a, b, dims=((1,), (0,))):
    return lax.dot_general(a, b, (dims, ((), ())), preferred_element_type=F32)


def by_head(x):
    return jnp.concatenate([x[:, :HD], x[:, HD:]], axis=0)


def by_lane(x):
    rows = x.shape[0] // 2
    return jnp.concatenate([x[:rows], x[rows:]], axis=1)


def fused(
    n_inst, nz, nx,
    q_hbm, home_hbm, lent_hbm, table_hbm, borrowed_hbm, lengths_hbm, weight_hbm,
    out_ref,
    q_v, home_v, lent_v, weight_v, table_s, borrowed_s, lengths_s,
    ask_out, ask_in, count_out, count_in, part_out, part_in, stat_out, stat_in, proj_out, proj_in,
    load_sem, send_sem, recv_sem, here_sem,
):
    n_tp = nz * nx
    slots = lent_v.shape[0]
    reqs = q_v.shape[0]
    me = lax.axis_index("inst")
    tp = lax.axis_index("tp")
    my_z, my_x = tp // nx, tp % nx
    scale = 1.0 / math.sqrt(HD)

    barrier = pltpu.get_barrier_semaphore()
    order = sorted(range(1, n_inst), key=lambda k: -min(k, n_inst - k))
    rounds = []
    step = 1
    while step <= nz // 2:
        rounds.append(sorted({step, nz - step}))
        step *= 2

    def along_z(d):
        return {"tp": (my_z + d) % nz * nx + my_x}

    for k in order:
        pl.semaphore_signal(barrier, 1, device_id={"inst": (me + k) % n_inst})
    for d in range(1, nx):
        pl.semaphore_signal(barrier, 1, device_id={"tp": my_z * nx + (my_x + d) % nx})
    for d in rounds[0] if rounds else []:
        pl.semaphore_signal(barrier, 1, device_id=along_z(d))
    greeted = n_inst - 1 + nx - 1 + (len(rounds[0]) if rounds else 0)

    def tell(i):
        for d in rounds[i] if i < len(rounds) else []:
            pl.semaphore_signal(here_sem.at[i], 1, device_id=along_z(d))

    def told(i):
        if i < len(rounds):
            pl.semaphore_wait(here_sem.at[i], len(rounds[i]))

    loads = []
    for i, (src, dst) in enumerate(
        [
            (table_hbm, table_s),
            (borrowed_hbm, borrowed_s),
            (lengths_hbm, lengths_s),
            (q_hbm, q_v),
            (home_hbm, home_v),
            (lent_hbm, lent_v),
            (weight_hbm, weight_v),
        ]
    ):
        copy = pltpu.make_async_copy(src, dst, load_sem.at[i])
        copy.start()
        loads.append(copy)

    for copy in loads[:4]:
        copy.wait()

    table = [[table_s[j, r] for j in range(RANKS)] for r in range(reqs)]
    length = [lengths_s[r] for r in range(reqs)]
    beyond = [
        length[r] - PAGE * sum((t >= 0).astype(I32) for t in table[r]) for r in range(reqs)
    ]
    shape = (reqs, 128)
    borrow = [column([borrowed_s[j, r] for r in range(reqs)], shape) for j in range(RANKS)]
    left = column(beyond, shape)
    counted = [jnp.clip(left - PAGE * j, 0, PAGE).astype(F32) for j in range(RANKS)]
    lane = lax.broadcasted_iota(I32, shape, 1)
    total_slots = n_inst * slots
    wanted, counts = [], []
    for base in range(0, total_slots, 128):
        hit = [b == lane + base for b in borrow]
        wanted.append((hit[0] | hit[1]).astype(F32))
        both = jnp.where(hit[0], counted[0], 0.0) + jnp.where(hit[1], counted[1], 0.0)
        counts.append(jnp.sum(both, axis=0, keepdims=True))
    wanted = jnp.concatenate(wanted, axis=1)[:, :total_slots].astype(BF16)
    counts = jnp.concatenate(counts, axis=1)
    q = q_v[...]
    asked = dot(wanted, q, ((0,), (0,))).astype(BF16)
    ask_out[...] = asked.reshape(n_inst, slots, 2 * HD)
    count_out[...] = counts
    ask_in[n_inst - 1] = ask_out[me]
    count_in[n_inst - 1] = counts

    pl.semaphore_wait(barrier, greeted)

    def send(src, dst, phase, to):
        pltpu.make_async_remote_copy(
            src_ref=src, dst_ref=dst, send_sem=send_sem.at[phase], recv_sem=recv_sem.at[phase], device_id=to
        ).start()

    n_chip = n_inst // 2

    def to_chips(chips, act):
        for y in chips:

            @pl.when(y != me // 2)
            def _():
                act(2 * y + 1)
                act(2 * y)

        act(me + 1 - 2 * (me % 2))

    def arrive(ref, count, phase):
        part = ref.at[pl.ds(0, count)]
        pltpu.make_async_copy(part, part, recv_sem.at[phase]).wait()

    def sent(ref, count, phase):
        part = ref.at[pl.ds(0, count)]
        pltpu.make_async_copy(part, part, send_sem.at[phase]).wait()

    def ask(to):
        place = (to - me - 1) % n_inst
        send(ask_out.at[to], ask_in.at[place], 0, {"inst": to})
        send(count_out, count_in.at[place], 1, {"inst": to})

    to_chips(sorted(range(n_chip), key=lambda y: abs(y - n_chip // 2)), ask)

    tell(0)

    row = lax.broadcasted_iota(I32, (2 * reqs, PAGE), 0) % reqs
    token = lax.broadcasted_iota(I32, (2 * reqs, PAGE), 1)
    q2 = by_head(q)
    loads[4].wait()
    scores = [jnp.zeros((2 * reqs, PAGE), F32) for _ in range(RANKS)]
    usable = [jnp.zeros((2 * reqs, PAGE), I32) for _ in range(RANKS)]
    for r in range(reqs):
        for j in range(RANKS):
            page = jnp.maximum(table[r][j], 0)
            s = dot(q2, home_v[page, 0, :, :HD], ((1,), (1,)))
            scores[j] = jnp.where(row == r, s, scores[j])
            here = jnp.where(table[r][j] >= 0, length[r] - PAGE * j, 0)
            usable[j] = jnp.where(row == r, here, usable[j])
    usable = [token < u for u in usable]
    scores = [jnp.where(u, s * scale, SENTINEL) for u, s in zip(usable, scores)]
    home_max = jnp.max(jnp.maximum(scores[0], scores[1]), axis=1, keepdims=True)
    home_w = [
        jnp.where(u, jnp.exp(s - home_max), 0.0).astype(BF16) for u, s in zip(usable, scores)
    ]
    home_total = sum(jnp.sum(w.astype(F32), axis=1, keepdims=True) for w in home_w)
    home_sum = jnp.zeros((2 * reqs, HD), F32)
    for r in range(reqs):
        o = 0.0
        for j in range(RANKS):
            page = jnp.maximum(table[r][j], 0)
            o = o + dot(home_w[j], home_v[page, 0, :, HD:])
        home_sum = jnp.where(row == r, o, home_sum)

    told(0)
    tell(1)

    loads[5].wait()
    arrive(ask_in, n_inst - 1, 0)
    arrive(count_in, n_inst - 1, 1)
    q_lent = ask_in[0]
    for k in range(1, n_inst):
        q_lent = q_lent + ask_in[k]
    q_lent = by_head(q_lent)
    count_row = jnp.sum(count_in[...], axis=0)
    wide = (slots, count_row.shape[1])
    mine = lax.broadcasted_iota(I32, wide, 1) == me * slots + lax.broadcasted_iota(I32, wide, 0)
    count_col = jnp.sum(jnp.where(mine, count_row, 0.0), axis=1, keepdims=True)
    count_col = jnp.concatenate([count_col, count_col], axis=0)
    lrow = lax.broadcasted_iota(I32, (2 * slots, PAGE), 0)
    lslot = lrow % slots
    llane = lax.broadcasted_iota(I32, (2 * slots, PAGE), 1)
    s = jnp.zeros((2 * slots, PAGE), F32)
    for p in range(slots):
        s = jnp.where(lslot == p, dot(q_lent, lent_v[p, 0, :, :HD], ((1,), (1,))), s)
    ok = llane < count_col.astype(I32)
    s = jnp.where(ok, s * scale, SENTINEL)
    lent_max = jnp.max(s, axis=1, keepdims=True)
    w = jnp.where(ok, jnp.exp(s - lent_max), 0.0).astype(BF16)
    lent_total = jnp.sum(w.astype(F32), axis=1, keepdims=True)
    o = jnp.zeros((2 * slots, HD), F32)
    for p in range(slots):
        o = jnp.where(lslot == p, dot(w, lent_v[p, 0, :, HD:]), o)
    part = by_lane(o).astype(BF16)
    stats = jnp.where(llane == lrow, lent_max, 0.0) + jnp.where(
        llane == lrow + 2 * slots, lent_total, 0.0
    )
    stats = jnp.sum(stats, axis=0, keepdims=True)
    part_out[...] = part
    stat_out[...] = stats
    part_in[n_inst - 1] = part
    stat_in[n_inst - 1] = stats
    def answer(to):
        place = (to - me - 1) % n_inst
        send(stat_out, stat_in.at[place], 3, {"inst": to})
        send(part_out, part_in.at[place], 2, {"inst": to})

    to_chips(sorted(range(n_chip), key=lambda y: min(y, n_chip - y)), answer)

    told(1)
    tell(2)

    two = jnp.concatenate(borrow, axis=0)
    gather = []
    for base in range(0, total_slots, 128):
        i = base + lax.broadcasted_iota(I32, two.shape, 1)
        name = (me - i // slots - 1) % n_inst * slots + i % slots
        gather.append((two == name).astype(F32))
    gather = jnp.concatenate(gather, axis=1)[:, :total_slots].astype(BF16)
    lane2 = lax.broadcasted_iota(I32, two.shape, 1)
    lender = ((me - lane2 - 1) % n_inst == two // slots) & (lane2 < n_inst) & (two >= 0)
    lender = lender[:, :n_inst].astype(F32).astype(BF16)
    slot = jnp.where(two >= 0, two % slots, -1)

    arrive(stat_in, n_inst - 1, 3)
    left_over = stat_in[...].reshape(n_inst, 128)
    found = jnp.zeros(two.shape, F32)
    for _ in range(3):
        piece = left_over.astype(BF16)
        found = found + dot(lender, piece)
        left_over = left_over - piece.astype(F32)
    present = two[:, :1] >= 0

    def pick(kind, absent):
        value = jnp.sum(jnp.where(lane2 == slot + kind * slots, found, 0.0), axis=1, keepdims=True)
        value = jnp.where((slot[:, :1] >= 0), value, absent)
        return [value[j * reqs : (j + 1) * reqs] for j in range(RANKS)]

    max0, max1 = pick(0, SENTINEL), pick(1, SENTINEL)
    tot0, tot1 = pick(2, 0.0), pick(3, 0.0)
    page_max = [jnp.concatenate([max0[j], max1[j]], axis=0) for j in range(RANKS)]
    page_total = [jnp.concatenate([tot0[j], tot1[j]], axis=0) for j in range(RANKS)]
    summit = jnp.maximum(home_max, jnp.maximum(page_max[0], page_max[1]))
    home_share = jnp.exp(home_max - summit)
    share = [jnp.exp(m - summit) for m in page_max]
    total = home_share * home_total + share[0] * page_total[0] + share[1] * page_total[1]
    total = jnp.maximum(total, 1.0)
    arrive(part_in, n_inst - 1, 2)
    got = dot(gather, part_in[...].reshape(total_slots, 2 * HD))
    attended = home_share * home_sum
    for j in range(RANKS):
        attended = attended + share[j] * by_head(got[j * reqs : (j + 1) * reqs])
    attended = by_lane(attended / total).astype(BF16)

    loads[6].wait()
    told(2)
    def project(z):
        start = pl.multiple_of(z * (nx * 128), nx * 128)
        block = dot(attended, weight_v[:, pl.ds(start, nx * 128)]).astype(BF16)
        for x in range(nx):
            proj_out[z * nx + x] = block[:, x * 128 : (x + 1) * 128]

    def hand_over(z, x):
        place = (z - my_z) % nz * nx + (x - my_x) % nx - 1
        send(proj_out.at[z * nx + x], proj_in.at[place], 4, {"tp": z * nx + x})

    for z in range(nz):
        project(z)

        @pl.when(z != my_z)
        def _():
            for x in range(nx):
                hand_over(z, x)

    for d in range(1, nx):
        hand_over(my_z, (my_x + d) % nx)
    result = proj_out[tp].astype(F32)
    arrive(proj_in, n_tp - 1, 4)
    result = result + jnp.sum(proj_in[...].astype(F32), axis=0)
    out_ref[...] = result.astype(out_ref.dtype)

    sent(ask_in, n_inst - 1, 0)
    sent(count_in, n_inst - 1, 1)
    sent(part_in, n_inst - 1, 2)
    sent(stat_in, n_inst - 1, 3)
    sent(proj_in, n_tp - 1, 4)


def shards(nx, queries, home_kv, lent_kv, page_table, borrowed, lengths, out_weight):
    n_inst, n_tp = lax.axis_size("inst"), lax.axis_size("tp")
    reqs = queries.shape[0]
    slots = lent_kv.shape[0]
    cols = out_weight.shape[1] // n_tp
    lanes = -(-n_inst * slots // 128) * 128
    return pl.pallas_call(
        functools.partial(fused, n_inst, n_tp // nx, nx),
        out_shape=jax.ShapeDtypeStruct((reqs, cols), BF16),
        in_specs=[pl.BlockSpec(memory_space=pltpu.HBM)] * 7,
        out_specs=pl.BlockSpec(memory_space=pltpu.VMEM),
        scratch_shapes=[
            pltpu.VMEM(queries.shape, BF16),
            pltpu.VMEM(home_kv.shape, BF16),
            pltpu.VMEM(lent_kv.shape, BF16),
            pltpu.VMEM(out_weight.shape, BF16),
            pltpu.SMEM(page_table.shape[::-1], I32),
            pltpu.SMEM(borrowed.shape[::-1], I32),
            pltpu.SMEM(lengths.shape, I32),
            pltpu.VMEM((n_inst, slots, 2 * HD), BF16),
            pltpu.VMEM((n_inst, slots, 2 * HD), BF16),
            pltpu.VMEM((1, lanes), F32),
            pltpu.VMEM((n_inst, 1, lanes), F32),
            pltpu.VMEM((slots, 2 * HD), BF16),
            pltpu.VMEM((n_inst, slots, 2 * HD), BF16),
            pltpu.VMEM((1, 128), F32),
            pltpu.VMEM((n_inst, 1, 128), F32),
            pltpu.VMEM((n_tp, reqs, cols), BF16),
            pltpu.VMEM((n_tp - 1, reqs, cols), BF16),
            pltpu.SemaphoreType.DMA((7,)),
            pltpu.SemaphoreType.DMA((5,)),
            pltpu.SemaphoreType.DMA((5,)),
            pltpu.SemaphoreType.REGULAR((3,)),
        ],
        compiler_params=pltpu.CompilerParams(
            collective_id=0, has_side_effects=True, vmem_limit_bytes=40 * 1024 * 1024
        ),
    )(*[pltpu.with_memory_space_constraint(x, pltpu.HBM) for x in (queries, home_kv, lent_kv, page_table.T, borrowed.T, lengths, out_weight)])


def solution(mesh):
    n_tp = mesh.shape["tp"]
    nx = 4 if n_tp % 4 == 0 else 1
    placed = (
        P("inst", "tp"),
        P("inst", "tp", None, None),
        P("inst", "tp", None, None),
        P("inst", None),
        P("inst", None),
        P("inst"),
        P("tp", None),
    )
    return jax.shard_map(
        functools.partial(shards, nx), mesh=mesh, in_specs=placed, out_specs=P("inst", "tp"), check_vma=False
    )
```

```python
import functools
import math

import jax
import jax.numpy as jnp
from jax import lax
from jax.experimental import pallas as pl
from jax.experimental.pallas import tpu as pltpu
from jax.sharding import PartitionSpec as P

HD = 128
PAGE = 128
RANKS = 2
SENTINEL = -1e30
F32 = jnp.float32
BF16 = jnp.bfloat16
I32 = jnp.int32


def column(values, shape):
    row = lax.broadcasted_iota(I32, shape, 0)
    out = jnp.full(shape, values[0], I32)
    for r in range(1, len(values)):
        out = jnp.where(row == r, values[r], out)
    return out


def dot(a, b, dims=((1,), (0,))):
    return lax.dot_general(a, b, (dims, ((), ())), preferred_element_type=F32)


def by_head(x):
    return jnp.concatenate([x[:, :HD], x[:, HD:]], axis=0)


def by_lane(x):
    rows = x.shape[0] // 2
    return jnp.concatenate([x[:rows], x[rows:]], axis=1)


def fused(
    n_inst, nz, nx,
    q_hbm, home_hbm, lent_hbm, table_hbm, borrowed_hbm, lengths_hbm, weight_hbm,
    out_ref,
    q_v, home_v, lent_v, weight_v, table_s, borrowed_s, lengths_s,
    ask_out, ask_in, count_out, count_in, part_out, part_in, stat_out, stat_in, proj_out, proj_in,
    keys_v, load_sem, send_sem, recv_sem, here_sem,
):
    n_tp = nz * nx
    slots = lent_v.shape[0]
    reqs = q_v.shape[0]
    me = lax.axis_index("inst")
    tp = lax.axis_index("tp")
    my_z, my_x = tp // nx, tp % nx
    scale = 1.0 / math.sqrt(HD)

    barrier = pltpu.get_barrier_semaphore()
    order = sorted(range(1, n_inst), key=lambda k: -min(k, n_inst - k))
    rounds = []
    step = 1
    while step <= nz // 2:
        rounds.append(sorted({step, nz - step}))
        step *= 2

    def along_z(d):
        return {"tp": (my_z + d) % nz * nx + my_x}

    for k in order:
        pl.semaphore_signal(barrier, 1, device_id={"inst": (me + k) % n_inst})
    for d in range(1, nx):
        pl.semaphore_signal(barrier, 1, device_id={"tp": my_z * nx + (my_x + d) % nx})
    for d in rounds[0] if rounds else []:
        pl.semaphore_signal(barrier, 1, device_id=along_z(d))
    greeted = n_inst - 1 + nx - 1 + (len(rounds[0]) if rounds else 0)

    def tell(i):
        for d in rounds[i] if i < len(rounds) else []:
            pl.semaphore_signal(here_sem.at[i], 1, device_id=along_z(d))

    def told(i):
        if i < len(rounds):
            pl.semaphore_wait(here_sem.at[i], len(rounds[i]))

    loads = []
    for i, (src, dst) in enumerate(
        [
            (table_hbm, table_s),
            (borrowed_hbm, borrowed_s),
            (lengths_hbm, lengths_s),
            (q_hbm, q_v),
            (home_hbm, home_v),
            (lent_hbm, lent_v),
            (weight_hbm, weight_v),
        ]
    ):
        copy = pltpu.make_async_copy(src, dst, load_sem.at[i])
        copy.start()
        loads.append(copy)

    for copy in loads[:4]:
        copy.wait()

    table = [[table_s[j, r] for j in range(RANKS)] for r in range(reqs)]
    length = [lengths_s[r] for r in range(reqs)]
    beyond = [
        length[r] - PAGE * sum((t >= 0).astype(I32) for t in table[r]) for r in range(reqs)
    ]
    shape = (reqs, 128)
    borrow = [column([borrowed_s[j, r] for r in range(reqs)], shape) for j in range(RANKS)]
    left = column(beyond, shape)
    counted = [jnp.clip(left - PAGE * j, 0, PAGE).astype(F32) for j in range(RANKS)]
    lane = lax.broadcasted_iota(I32, shape, 1)
    total_slots = n_inst * slots
    wanted, counts = [], []
    for base in range(0, total_slots, 128):
        hit = [b == lane + base for b in borrow]
        wanted.append((hit[0] | hit[1]).astype(F32))
        both = jnp.where(hit[0], counted[0], 0.0) + jnp.where(hit[1], counted[1], 0.0)
        counts.append(jnp.sum(both, axis=0, keepdims=True))
    wanted = jnp.concatenate(wanted, axis=1)[:, :total_slots].astype(BF16)
    counts = jnp.concatenate(counts, axis=1)
    q = q_v[...]
    asked = dot(wanted, q, ((0,), (0,))).astype(BF16)
    ask_out[...] = asked.reshape(n_inst, slots, 2 * HD)
    count_out[...] = counts
    ask_in[n_inst - 1] = ask_out[me]
    count_in[n_inst - 1] = counts

    pl.semaphore_wait(barrier, greeted)

    def send(src, dst, phase, to):
        pltpu.make_async_remote_copy(
            src_ref=src, dst_ref=dst, send_sem=send_sem.at[phase], recv_sem=recv_sem.at[phase], device_id=to
        ).start()

    n_chip = n_inst // 2

    def to_chips(chips, act):
        for y in chips:

            @pl.when(y != me // 2)
            def _():
                act(2 * y + 1 - me % 2)
                act(2 * y + me % 2)

        act(me + 1 - 2 * (me % 2))

    def arrive(ref, count, phase):
        part = ref.at[pl.ds(0, count)]
        pltpu.make_async_copy(part, part, recv_sem.at[phase]).wait()

    def sent(ref, count, phase):
        part = ref.at[pl.ds(0, count)]
        pltpu.make_async_copy(part, part, send_sem.at[phase]).wait()

    def ask(to):
        place = (to - me - 1) % n_inst
        send(ask_out.at[to], ask_in.at[place], 0, {"inst": to})
        send(count_out, count_in.at[place], 1, {"inst": to})

    to_chips(sorted(range(n_chip), key=lambda y: abs(y - n_chip // 2)), ask)

    tell(0)

    row = lax.broadcasted_iota(I32, (2 * reqs, PAGE), 0) % reqs
    token = lax.broadcasted_iota(I32, (2 * reqs, PAGE), 1)
    q2 = by_head(q)
    loads[4].wait()
    scores = [jnp.zeros((2 * reqs, PAGE), F32) for _ in range(RANKS)]
    usable = [jnp.zeros((2 * reqs, PAGE), I32) for _ in range(RANKS)]
    for r in range(reqs):
        for j in range(RANKS):
            page = jnp.maximum(table[r][j], 0)
            s = dot(q2, home_v[page, 0, :, :HD], ((1,), (1,)))
            scores[j] = jnp.where(row == r, s, scores[j])
            here = jnp.where(table[r][j] >= 0, length[r] - PAGE * j, 0)
            usable[j] = jnp.where(row == r, here, usable[j])
    usable = [token < u for u in usable]
    scores = [jnp.where(u, s * scale, SENTINEL) for u, s in zip(usable, scores)]
    home_max = jnp.max(jnp.maximum(scores[0], scores[1]), axis=1, keepdims=True)
    home_w = [
        jnp.where(u, jnp.exp(s - home_max), 0.0).astype(BF16) for u, s in zip(usable, scores)
    ]
    home_total = sum(jnp.sum(w.astype(F32), axis=1, keepdims=True) for w in home_w)
    home_sum = jnp.zeros((2 * reqs, HD), F32)
    for r in range(reqs):
        o = 0.0
        for j in range(RANKS):
            page = jnp.maximum(table[r][j], 0)
            o = o + dot(home_w[j], home_v[page, 0, :, HD:])
        home_sum = jnp.where(row == r, o, home_sum)

    told(0)
    tell(1)

    loads[5].wait()
    for p in range(slots):
        keys_v[p * HD : (p + 1) * HD] = lent_v[p, 0, :, :HD].T
    lrow = lax.broadcasted_iota(I32, (2 * slots, PAGE), 0)
    llane = lax.broadcasted_iota(I32, (2 * slots, PAGE), 1)
    own = [(lrow % slots == p).astype(F32).astype(BF16) for p in range(slots)]

    def spread(x):
        return jnp.concatenate([x * o for o in own], axis=1)

    arrive(ask_in, n_inst - 1, 0)
    arrive(count_in, n_inst - 1, 1)
    q_lent = ask_in[0]
    for k in range(1, n_inst):
        q_lent = q_lent + ask_in[k]
    q_lent = by_head(q_lent)
    count_row = jnp.sum(count_in[...], axis=0)
    wide = (slots, count_row.shape[1])
    mine = lax.broadcasted_iota(I32, wide, 1) == me * slots + lax.broadcasted_iota(I32, wide, 0)
    count_col = jnp.sum(jnp.where(mine, count_row, 0.0), axis=1, keepdims=True)
    count_col = jnp.concatenate([count_col, count_col], axis=0)
    s = dot(spread(q_lent), keys_v[...])
    ok = llane < count_col.astype(I32)
    s = jnp.where(ok, s * scale, SENTINEL)
    lent_max = jnp.max(s, axis=1, keepdims=True)
    w = jnp.where(ok, jnp.exp(s - lent_max), 0.0).astype(BF16)
    lent_total = jnp.sum(w.astype(F32), axis=1, keepdims=True)
    o = dot(spread(w), lent_v[:, 0, :, HD:].reshape(slots * PAGE, HD))
    part = by_lane(o).astype(BF16)
    stats = jnp.where(llane == lrow, lent_max, 0.0) + jnp.where(
        llane == lrow + 2 * slots, lent_total, 0.0
    )
    stats = jnp.sum(stats, axis=0, keepdims=True)
    part_out[...] = part
    stat_out[...] = stats
    part_in[n_inst - 1] = part
    stat_in[n_inst - 1] = stats
    def answer(to):
        place = (to - me - 1) % n_inst
        send(stat_out, stat_in.at[place], 3, {"inst": to})
        send(part_out, part_in.at[place], 2, {"inst": to})

    to_chips(sorted(range(n_chip), key=lambda y: min(y, n_chip + 1 - y)), answer)

    told(1)
    tell(2)

    two = jnp.concatenate(borrow, axis=0)
    gather = []
    for base in range(0, total_slots, 128):
        i = base + lax.broadcasted_iota(I32, two.shape, 1)
        name = (me - i // slots - 1) % n_inst * slots + i % slots
        gather.append((two == name).astype(F32))
    gather = jnp.concatenate(gather, axis=1)[:, :total_slots].astype(BF16)
    lane2 = lax.broadcasted_iota(I32, two.shape, 1)
    lender = ((me - lane2 - 1) % n_inst == two // slots) & (lane2 < n_inst) & (two >= 0)
    lender = lender[:, :n_inst].astype(F32).astype(BF16)
    slot = jnp.where(two >= 0, two % slots, -1)

    arrive(stat_in, n_inst - 1, 3)
    left_over = stat_in[...].reshape(n_inst, 128)
    found = jnp.zeros(two.shape, F32)
    for _ in range(3):
        piece = left_over.astype(BF16)
        found = found + dot(lender, piece)
        left_over = left_over - piece.astype(F32)
    present = two[:, :1] >= 0

    def pick(kind, absent):
        value = jnp.sum(jnp.where(lane2 == slot + kind * slots, found, 0.0), axis=1, keepdims=True)
        value = jnp.where((slot[:, :1] >= 0), value, absent)
        return [value[j * reqs : (j + 1) * reqs] for j in range(RANKS)]

    max0, max1 = pick(0, SENTINEL), pick(1, SENTINEL)
    tot0, tot1 = pick(2, 0.0), pick(3, 0.0)
    page_max = [jnp.concatenate([max0[j], max1[j]], axis=0) for j in range(RANKS)]
    page_total = [jnp.concatenate([tot0[j], tot1[j]], axis=0) for j in range(RANKS)]
    summit = jnp.maximum(home_max, jnp.maximum(page_max[0], page_max[1]))
    home_share = jnp.exp(home_max - summit)
    share = [jnp.exp(m - summit) for m in page_max]
    total = home_share * home_total + share[0] * page_total[0] + share[1] * page_total[1]
    total = jnp.maximum(total, 1.0)
    arrive(part_in, n_inst - 1, 2)
    got = dot(gather, part_in[...].reshape(total_slots, 2 * HD))
    attended = home_share * home_sum
    for j in range(RANKS):
        attended = attended + share[j] * by_head(got[j * reqs : (j + 1) * reqs])
    attended = by_lane(attended / total).astype(BF16)

    loads[6].wait()
    told(2)
    def project(z):
        start = pl.multiple_of(z * (nx * 128), nx * 128)
        block = dot(attended, weight_v[:, pl.ds(start, nx * 128)]).astype(BF16)
        for x in range(nx):
            proj_out[z * nx + x] = block[:, x * 128 : (x + 1) * 128]

    def hand_over(z, x):
        place = (z - my_z) % nz * nx + (x - my_x) % nx - 1
        send(proj_out.at[z * nx + x], proj_in.at[place], 4, {"tp": z * nx + x})

    for z in range(nz):
        project(z)

        @pl.when(z != my_z)
        def _():
            for x in range(nx):
                hand_over(z, x)

    for d in range(1, nx):
        hand_over(my_z, (my_x + d) % nx)
    result = proj_out[tp].astype(F32)
    arrive(proj_in, n_tp - 1, 4)
    result = result + jnp.sum(proj_in[...].astype(F32), axis=0)
    out_ref[...] = result.astype(out_ref.dtype)

    sent(ask_in, n_inst - 1, 0)
    sent(count_in, n_inst - 1, 1)
    sent(part_in, n_inst - 1, 2)
    sent(stat_in, n_inst - 1, 3)
    sent(proj_in, n_tp - 1, 4)


def shards(nx, queries, home_kv, lent_kv, page_table, borrowed, lengths, out_weight):
    n_inst, n_tp = lax.axis_size("inst"), lax.axis_size("tp")
    reqs = queries.shape[0]
    slots = lent_kv.shape[0]
    cols = out_weight.shape[1] // n_tp
    lanes = -(-n_inst * slots // 128) * 128
    return pl.pallas_call(
        functools.partial(fused, n_inst, n_tp // nx, nx),
        out_shape=jax.ShapeDtypeStruct((reqs, cols), BF16),
        in_specs=[pl.BlockSpec(memory_space=pltpu.HBM)] * 7,
        out_specs=pl.BlockSpec(memory_space=pltpu.VMEM),
        scratch_shapes=[
            pltpu.VMEM(queries.shape, BF16),
            pltpu.VMEM(home_kv.shape, BF16),
            pltpu.VMEM(lent_kv.shape, BF16),
            pltpu.VMEM(out_weight.shape, BF16),
            pltpu.SMEM(page_table.shape[::-1], I32),
            pltpu.SMEM(borrowed.shape[::-1], I32),
            pltpu.SMEM(lengths.shape, I32),
            pltpu.VMEM((n_inst, slots, 2 * HD), BF16),
            pltpu.VMEM((n_inst, slots, 2 * HD), BF16),
            pltpu.VMEM((1, lanes), F32),
            pltpu.VMEM((n_inst, 1, lanes), F32),
            pltpu.VMEM((slots, 2 * HD), BF16),
            pltpu.VMEM((n_inst, slots, 2 * HD), BF16),
            pltpu.VMEM((1, 128), F32),
            pltpu.VMEM((n_inst, 1, 128), F32),
            pltpu.VMEM((n_tp, reqs, cols), BF16),
            pltpu.VMEM((n_tp - 1, reqs, cols), BF16),
            pltpu.VMEM((slots * HD, PAGE), BF16),
            pltpu.SemaphoreType.DMA((7,)),
            pltpu.SemaphoreType.DMA((5,)),
            pltpu.SemaphoreType.DMA((5,)),
            pltpu.SemaphoreType.REGULAR((3,)),
        ],
        compiler_params=pltpu.CompilerParams(
            collective_id=0, has_side_effects=True, vmem_limit_bytes=40 * 1024 * 1024
        ),
    )(*[pltpu.with_memory_space_constraint(x, pltpu.HBM) for x in (queries, home_kv, lent_kv, page_table.T, borrowed.T, lengths, out_weight)])


def solution(mesh):
    n_tp = mesh.shape["tp"]
    nx = 4 if n_tp % 4 == 0 else 1
    placed = (
        P("inst", "tp"),
        P("inst", "tp", None, None),
        P("inst", "tp", None, None),
        P("inst", None),
        P("inst", None),
        P("inst"),
        P("tp", None),
    )
    return jax.shard_map(
        functools.partial(shards, nx), mesh=mesh, in_specs=placed, out_specs=P("inst", "tp"), check_vma=False
    )
```

```python
import functools
import math

import jax
import jax.numpy as jnp
from jax import lax
from jax.experimental import pallas as pl
from jax.experimental.pallas import tpu as pltpu
from jax.sharding import PartitionSpec as P

HD = 128
PAGE = 128
RANKS = 2
SENTINEL = -1e30
F32 = jnp.float32
BF16 = jnp.bfloat16
I32 = jnp.int32


def column(values, shape):
    row = lax.broadcasted_iota(I32, shape, 0)
    out = jnp.full(shape, values[0], I32)
    for r in range(1, len(values)):
        out = jnp.where(row == r, values[r], out)
    return out


def dot(a, b, dims=((1,), (0,))):
    return lax.dot_general(a, b, (dims, ((), ())), preferred_element_type=F32)


def by_head(x):
    return jnp.concatenate([x[:, :HD], x[:, HD:]], axis=0)


def by_lane(x):
    rows = x.shape[0] // 2
    return jnp.concatenate([x[:rows], x[rows:]], axis=1)


def fused(
    n_inst, nz, nx,
    q_hbm, home_hbm, lent_hbm, table_hbm, borrowed_hbm, lengths_hbm, weight_hbm,
    out_ref,
    q_v, home_v, lent_v, weight_v, table_s, borrowed_s, lengths_s,
    ask_out, ask_in, ask_relay, count_out, count_in, count_relay, count_sum, part_out, part_in, stat_out, stat_in, proj_out, proj_in,
    keys_v, load_sem, send_sem, recv_sem, here_sem,
):
    n_tp = nz * nx
    slots = lent_v.shape[0]
    reqs = q_v.shape[0]
    me = lax.axis_index("inst")
    tp = lax.axis_index("tp")
    my_z, my_x = tp // nx, tp % nx
    my_y, my_c = me // 2, me % 2
    n_chip = n_inst // 2
    half = n_chip // 2
    near = [d for d in range(1, n_chip) if d != half]
    n_near = len(near)
    far_first = sorted(range(n_near), key=lambda p: -min(near[p], n_chip - near[p]))
    sibling = me + 1 - 2 * my_c

    def chip_at(dy, other=0):
        return (my_y + dy) % n_chip * 2 + (my_c + other - 2 * my_c * other)
    scale = 1.0 / math.sqrt(HD)

    barrier = pltpu.get_barrier_semaphore()
    order = sorted(range(1, n_inst), key=lambda k: -min(k, n_inst - k))
    rounds = []
    step = 1
    while step <= nz // 2:
        rounds.append(sorted({step, nz - step}))
        step *= 2

    def along_z(d):
        return {"tp": (my_z + d) % nz * nx + my_x}

    for k in order:
        pl.semaphore_signal(barrier, 1, device_id={"inst": (me + k) % n_inst})
    for d in range(1, nx):
        pl.semaphore_signal(barrier, 1, device_id={"tp": my_z * nx + (my_x + d) % nx})
    for d in rounds[0] if rounds else []:
        pl.semaphore_signal(barrier, 1, device_id=along_z(d))
    greeted = n_inst - 1 + nx - 1 + (len(rounds[0]) if rounds else 0)

    def tell(i):
        for d in rounds[i] if i < len(rounds) else []:
            pl.semaphore_signal(here_sem.at[i], 1, device_id=along_z(d))

    def told(i):
        if i < len(rounds):
            pl.semaphore_wait(here_sem.at[i], len(rounds[i]))

    loads = []
    for i, (src, dst) in enumerate(
        [
            (table_hbm, table_s),
            (borrowed_hbm, borrowed_s),
            (lengths_hbm, lengths_s),
            (q_hbm, q_v),
            (home_hbm, home_v),
            (lent_hbm, lent_v),
            (weight_hbm, weight_v),
        ]
    ):
        copy = pltpu.make_async_copy(src, dst, load_sem.at[i])
        copy.start()
        loads.append(copy)

    for copy in loads[:4]:
        copy.wait()

    table = [[table_s[j, r] for j in range(RANKS)] for r in range(reqs)]
    length = [lengths_s[r] for r in range(reqs)]
    beyond = [
        length[r] - PAGE * sum((t >= 0).astype(I32) for t in table[r]) for r in range(reqs)
    ]
    shape = (reqs, 128)
    borrow = [column([borrowed_s[j, r] for r in range(reqs)], shape) for j in range(RANKS)]
    left = column(beyond, shape)
    counted = [jnp.clip(left - PAGE * j, 0, PAGE).astype(F32) for j in range(RANKS)]
    lane = lax.broadcasted_iota(I32, shape, 1)
    total_slots = n_inst * slots
    wanted, counts = [], []
    for base in range(0, total_slots, 128):
        block = (lane + base) // slots
        other, place = block // n_chip, block % n_chip
        dy = jnp.where(place < half - 1, place + 1, place + 2)
        dy = jnp.where(place < n_near, dy, jnp.where(place == n_near, half, 0))
        name = chip_at(dy, other) * slots + lane % slots
        wanted.append(((borrow[0] == name) | (borrow[1] == name)).astype(F32))
        hit = [b == lane + base for b in borrow]
        both = jnp.where(hit[0], counted[0], 0.0) + jnp.where(hit[1], counted[1], 0.0)
        counts.append(jnp.sum(both, axis=0, keepdims=True))
    wanted = jnp.concatenate(wanted, axis=1)[:, :total_slots].astype(BF16)
    counts = jnp.concatenate(counts, axis=1)
    q = q_v[...]
    asked = dot(wanted, q, ((0,), (0,))).astype(BF16)
    ask_out[...] = asked.reshape(n_inst, slots, 2 * HD)
    count_out[...] = counts
    ask_in[n_near + 3] = ask_out[n_near + 1]

    pl.semaphore_wait(barrier, greeted)

    def send(src, dst, phase, to):
        pltpu.make_async_remote_copy(
            src_ref=src, dst_ref=dst, send_sem=send_sem.at[phase], recv_sem=recv_sem.at[phase], device_id=to
        ).start()

    def to_chips(chips, act):
        for y in chips:

            @pl.when(y != me // 2)
            def _():
                act(2 * y + 1 - me % 2)
                act(2 * y + me % 2)

        act(me + 1 - 2 * (me % 2))

    def arrive(ref, count, phase):
        part = ref.at[pl.ds(0, count)]
        pltpu.make_async_copy(part, part, recv_sem.at[phase]).wait()

    def sent(ref, count, phase):
        part = ref.at[pl.ds(0, count)]
        pltpu.make_async_copy(part, part, send_sem.at[phase]).wait()

    over = {"inst": sibling}
    send(ask_out.at[pl.ds(n_chip, n_near)], ask_relay, 5, over)
    send(count_out, count_relay, 6, over)
    for other in range(2):
        to = {"inst": chip_at(half, other)}
        send(ask_out.at[other * n_chip + n_near], ask_in.at[n_near + other], 0, to)
        send(count_out, count_in.at[n_near + other], 1, to)
    send(ask_out.at[n_chip + n_near + 1], ask_in.at[n_near + 2], 0, over)
    arrive(ask_relay, n_near, 5)
    arrive(count_relay, 1, 6)
    for p in range(n_near):
        ask_out[p] = ask_out[p] + ask_relay[p]
    count_sum[...] = counts + count_relay[...]
    for p in far_first:
        to = {"inst": chip_at(near[p])}
        send(ask_out.at[p], ask_in.at[p], 0, to)
        send(count_sum, count_in.at[p], 1, to)
    tell(0)

    row = lax.broadcasted_iota(I32, (2 * reqs, PAGE), 0) % reqs
    token = lax.broadcasted_iota(I32, (2 * reqs, PAGE), 1)
    q2 = by_head(q)
    loads[4].wait()
    scores = [jnp.zeros((2 * reqs, PAGE), F32) for _ in range(RANKS)]
    usable = [jnp.zeros((2 * reqs, PAGE), I32) for _ in range(RANKS)]
    for r in range(reqs):
        for j in range(RANKS):
            page = jnp.maximum(table[r][j], 0)
            s = dot(q2, home_v[page, 0, :, :HD], ((1,), (1,)))
            scores[j] = jnp.where(row == r, s, scores[j])
            here = jnp.where(table[r][j] >= 0, length[r] - PAGE * j, 0)
            usable[j] = jnp.where(row == r, here, usable[j])
    usable = [token < u for u in usable]
    scores = [jnp.where(u, s * scale, SENTINEL) for u, s in zip(usable, scores)]
    home_max = jnp.max(jnp.maximum(scores[0], scores[1]), axis=1, keepdims=True)
    home_w = [
        jnp.where(u, jnp.exp(s - home_max), 0.0).astype(BF16) for u, s in zip(usable, scores)
    ]
    home_total = sum(jnp.sum(w.astype(F32), axis=1, keepdims=True) for w in home_w)
    home_sum = jnp.zeros((2 * reqs, HD), F32)
    for r in range(reqs):
        o = 0.0
        for j in range(RANKS):
            page = jnp.maximum(table[r][j], 0)
            o = o + dot(home_w[j], home_v[page, 0, :, HD:])
        home_sum = jnp.where(row == r, o, home_sum)

    told(0)
    tell(1)

    loads[5].wait()
    for p in range(slots):
        keys_v[p * HD : (p + 1) * HD] = lent_v[p, 0, :, :HD].T
    lrow = lax.broadcasted_iota(I32, (2 * slots, PAGE), 0)
    llane = lax.broadcasted_iota(I32, (2 * slots, PAGE), 1)
    own = [(lrow % slots == p).astype(F32).astype(BF16) for p in range(slots)]

    def spread(x):
        return jnp.concatenate([x * o for o in own], axis=1)

    arrive(ask_in, n_near + 3, 0)
    arrive(count_in, n_near + 2, 1)
    q_lent = ask_in[0]
    for k in range(1, n_near + 4):
        q_lent = q_lent + ask_in[k]
    q_lent = by_head(q_lent)
    count_row = jnp.sum(count_in[...], axis=0) + counts + count_relay[...]
    wide = (slots, count_row.shape[1])
    mine = lax.broadcasted_iota(I32, wide, 1) == me * slots + lax.broadcasted_iota(I32, wide, 0)
    count_col = jnp.sum(jnp.where(mine, count_row, 0.0), axis=1, keepdims=True)
    count_col = jnp.concatenate([count_col, count_col], axis=0)
    s = dot(spread(q_lent), keys_v[...])
    ok = llane < count_col.astype(I32)
    s = jnp.where(ok, s * scale, SENTINEL)
    lent_max = jnp.max(s, axis=1, keepdims=True)
    w = jnp.where(ok, jnp.exp(s - lent_max), 0.0).astype(BF16)
    lent_total = jnp.sum(w.astype(F32), axis=1, keepdims=True)
    o = dot(spread(w), lent_v[:, 0, :, HD:].reshape(slots * PAGE, HD))
    part = by_lane(o).astype(BF16)
    stats = jnp.where(llane == lrow, lent_max, 0.0) + jnp.where(
        llane == lrow + 2 * slots, lent_total, 0.0
    )
    stats = jnp.sum(stats, axis=0, keepdims=True)
    part_out[...] = part
    stat_out[...] = stats
    part_in[n_inst - 1] = part
    stat_in[n_inst - 1] = stats
    def answer(to):
        place = (to - me - 1) % n_inst
        send(stat_out, stat_in.at[place], 3, {"inst": to})
        send(part_out, part_in.at[place], 2, {"inst": to})

    to_chips(sorted(range(n_chip), key=lambda y: min(y, n_chip + 1 - y)), answer)

    told(1)
    tell(2)

    two = jnp.concatenate(borrow, axis=0)
    gather = []
    for base in range(0, total_slots, 128):
        i = base + lax.broadcasted_iota(I32, two.shape, 1)
        name = (me - i // slots - 1) % n_inst * slots + i % slots
        gather.append((two == name).astype(F32))
    gather = jnp.concatenate(gather, axis=1)[:, :total_slots].astype(BF16)
    lane2 = lax.broadcasted_iota(I32, two.shape, 1)
    lender = ((me - lane2 - 1) % n_inst == two // slots) & (lane2 < n_inst) & (two >= 0)
    lender = lender[:, :n_inst].astype(F32).astype(BF16)
    slot = jnp.where(two >= 0, two % slots, -1)

    arrive(stat_in, n_inst - 1, 3)
    left_over = stat_in[...].reshape(n_inst, 128)
    found = jnp.zeros(two.shape, F32)
    for _ in range(3):
        piece = left_over.astype(BF16)
        found = found + dot(lender, piece)
        left_over = left_over - piece.astype(F32)
    present = two[:, :1] >= 0

    def pick(kind, absent):
        value = jnp.sum(jnp.where(lane2 == slot + kind * slots, found, 0.0), axis=1, keepdims=True)
        value = jnp.where((slot[:, :1] >= 0), value, absent)
        return [value[j * reqs : (j + 1) * reqs] for j in range(RANKS)]

    max0, max1 = pick(0, SENTINEL), pick(1, SENTINEL)
    tot0, tot1 = pick(2, 0.0), pick(3, 0.0)
    page_max = [jnp.concatenate([max0[j], max1[j]], axis=0) for j in range(RANKS)]
    page_total = [jnp.concatenate([tot0[j], tot1[j]], axis=0) for j in range(RANKS)]
    summit = jnp.maximum(home_max, jnp.maximum(page_max[0], page_max[1]))
    home_share = jnp.exp(home_max - summit)
    share = [jnp.exp(m - summit) for m in page_max]
    total = home_share * home_total + share[0] * page_total[0] + share[1] * page_total[1]
    total = jnp.maximum(total, 1.0)
    arrive(part_in, n_inst - 1, 2)
    got = dot(gather, part_in[...].reshape(total_slots, 2 * HD))
    attended = home_share * home_sum
    for j in range(RANKS):
        attended = attended + share[j] * by_head(got[j * reqs : (j + 1) * reqs])
    attended = by_lane(attended / total).astype(BF16)

    loads[6].wait()
    told(2)
    def project(z):
        start = pl.multiple_of(z * (nx * 128), nx * 128)
        block = dot(attended, weight_v[:, pl.ds(start, nx * 128)]).astype(BF16)
        for x in range(nx):
            proj_out[z * nx + x] = block[:, x * 128 : (x + 1) * 128]

    def hand_over(z, x):
        place = (z - my_z) % nz * nx + (x - my_x) % nx - 1
        send(proj_out.at[z * nx + x], proj_in.at[place], 4, {"tp": z * nx + x})

    for z in range(nz):
        project(z)

        @pl.when(z != my_z)
        def _():
            for x in range(nx):
                hand_over(z, x)

    for d in range(1, nx):
        hand_over(my_z, (my_x + d) % nx)
    result = proj_out[tp].astype(F32)
    arrive(proj_in, n_tp - 1, 4)
    result = result + jnp.sum(proj_in[...].astype(F32), axis=0)
    out_ref[...] = result.astype(out_ref.dtype)

    sent(ask_in, n_near + 3, 0)
    sent(count_in, n_near + 2, 1)
    sent(ask_relay, n_near, 5)
    sent(count_relay, 1, 6)
    sent(part_in, n_inst - 1, 2)
    sent(stat_in, n_inst - 1, 3)
    sent(proj_in, n_tp - 1, 4)


def shards(nx, queries, home_kv, lent_kv, page_table, borrowed, lengths, out_weight):
    n_inst, n_tp = lax.axis_size("inst"), lax.axis_size("tp")
    reqs = queries.shape[0]
    slots = lent_kv.shape[0]
    cols = out_weight.shape[1] // n_tp
    lanes = -(-n_inst * slots // 128) * 128
    return pl.pallas_call(
        functools.partial(fused, n_inst, n_tp // nx, nx),
        out_shape=jax.ShapeDtypeStruct((reqs, cols), BF16),
        in_specs=[pl.BlockSpec(memory_space=pltpu.HBM)] * 7,
        out_specs=pl.BlockSpec(memory_space=pltpu.VMEM),
        scratch_shapes=[
            pltpu.VMEM(queries.shape, BF16),
            pltpu.VMEM(home_kv.shape, BF16),
            pltpu.VMEM(lent_kv.shape, BF16),
            pltpu.VMEM(out_weight.shape, BF16),
            pltpu.SMEM(page_table.shape[::-1], I32),
            pltpu.SMEM(borrowed.shape[::-1], I32),
            pltpu.SMEM(lengths.shape, I32),
            pltpu.VMEM((n_inst, slots, 2 * HD), BF16),
            pltpu.VMEM((n_inst // 2 + 2, slots, 2 * HD), BF16),
            pltpu.VMEM((n_inst // 2 - 2, slots, 2 * HD), BF16),
            pltpu.VMEM((1, lanes), F32),
            pltpu.VMEM((n_inst // 2, 1, lanes), F32),
            pltpu.VMEM((1, lanes), F32),
            pltpu.VMEM((1, lanes), F32),
            pltpu.VMEM((slots, 2 * HD), BF16),
            pltpu.VMEM((n_inst, slots, 2 * HD), BF16),
            pltpu.VMEM((1, 128), F32),
            pltpu.VMEM((n_inst, 1, 128), F32),
            pltpu.VMEM((n_tp, reqs, cols), BF16),
            pltpu.VMEM((n_tp - 1, reqs, cols), BF16),
            pltpu.VMEM((slots * HD, PAGE), BF16),
            pltpu.SemaphoreType.DMA((7,)),
            pltpu.SemaphoreType.DMA((7,)),
            pltpu.SemaphoreType.DMA((7,)),
            pltpu.SemaphoreType.REGULAR((3,)),
        ],
        compiler_params=pltpu.CompilerParams(
            collective_id=0, has_side_effects=True, vmem_limit_bytes=40 * 1024 * 1024
        ),
    )(*[pltpu.with_memory_space_constraint(x, pltpu.HBM) for x in (queries, home_kv, lent_kv, page_table.T, borrowed.T, lengths, out_weight)])


def solution(mesh):
    n_tp = mesh.shape["tp"]
    nx = 4 if n_tp % 4 == 0 else 1
    placed = (
        P("inst", "tp"),
        P("inst", "tp", None, None),
        P("inst", "tp", None, None),
        P("inst", None),
        P("inst", None),
        P("inst"),
        P("tp", None),
    )
    return jax.shard_map(
        functools.partial(shards, nx), mesh=mesh, in_specs=placed, out_specs=P("inst", "tp"), check_vma=False
    )
```

```python
import functools
import math

import jax
import jax.numpy as jnp
from jax import lax
from jax.experimental import pallas as pl
from jax.experimental.pallas import tpu as pltpu
from jax.sharding import PartitionSpec as P

HD = 128
PAGE = 128
RANKS = 2
SENTINEL = -1e30
F32 = jnp.float32
BF16 = jnp.bfloat16
I32 = jnp.int32


def column(values, shape):
    row = lax.broadcasted_iota(I32, shape, 0)
    out = jnp.full(shape, values[0], I32)
    for r in range(1, len(values)):
        out = jnp.where(row == r, values[r], out)
    return out


def dot(a, b, dims=((1,), (0,))):
    return lax.dot_general(a, b, (dims, ((), ())), preferred_element_type=F32)


def by_head(x):
    return jnp.concatenate([x[:, :HD], x[:, HD:]], axis=0)


def by_lane(x):
    rows = x.shape[0] // 2
    return jnp.concatenate([x[:rows], x[rows:]], axis=1)


def fused(
    n_inst, nz, nx,
    q_hbm, home_hbm, lent_hbm, table_hbm, borrowed_hbm, lengths_hbm, weight_hbm,
    out_ref,
    q_v, home_v, lent_v, weight_v, table_s, borrowed_s, lengths_s,
    ask_out, ask_in, ask_relay, count_out, count_in, count_relay, count_sum, part_out, part_in, stat_out, stat_in, proj_out, proj_in,
    keys_v, load_sem, send_sem, recv_sem, here_sem,
):
    n_tp = nz * nx
    slots = lent_v.shape[0]
    reqs = q_v.shape[0]
    me = lax.axis_index("inst")
    tp = lax.axis_index("tp")
    my_z, my_x = tp // nx, tp % nx
    my_y, my_c = me // 2, me % 2
    n_chip = n_inst // 2
    half = n_chip // 2
    near = [d for d in range(1, n_chip) if d != half]
    n_near = len(near)
    far_first = sorted(range(n_near), key=lambda p: -min(near[p], n_chip - near[p]))
    sibling = me + 1 - 2 * my_c

    def chip_at(dy, other=0):
        return (my_y + dy) % n_chip * 2 + (my_c + other - 2 * my_c * other)
    scale = 1.0 / math.sqrt(HD)

    barrier = pltpu.get_barrier_semaphore()
    order = sorted(range(1, n_inst), key=lambda k: -min(k, n_inst - k))
    rounds = []
    step = 1
    while step <= nz // 2:
        rounds.append(sorted({step, nz - step}))
        step *= 2

    def along_z(d):
        return {"tp": (my_z + d) % nz * nx + my_x}

    for k in order:
        pl.semaphore_signal(barrier, 1, device_id={"inst": (me + k) % n_inst})
    for d in range(1, nx):
        pl.semaphore_signal(barrier, 1, device_id={"tp": my_z * nx + (my_x + d) % nx})
    for d in rounds[0] if rounds else []:
        pl.semaphore_signal(barrier, 1, device_id=along_z(d))
    greeted = n_inst - 1 + nx - 1 + (len(rounds[0]) if rounds else 0)

    def tell(i):
        for d in rounds[i] if i < len(rounds) else []:
            pl.semaphore_signal(here_sem.at[i], 1, device_id=along_z(d))

    def told(i):
        if i < len(rounds):
            pl.semaphore_wait(here_sem.at[i], len(rounds[i]))

    loads = []
    for i, (src, dst) in enumerate(
        [
            (table_hbm, table_s),
            (borrowed_hbm, borrowed_s),
            (lengths_hbm, lengths_s),
            (q_hbm, q_v),
            (home_hbm, home_v),
            (lent_hbm, lent_v),
            (weight_hbm, weight_v),
        ]
    ):
        copy = pltpu.make_async_copy(src, dst, load_sem.at[i])
        copy.start()
        loads.append(copy)

    for copy in loads[:4]:
        copy.wait()

    table = [[table_s[j, r] for j in range(RANKS)] for r in range(reqs)]
    length = [lengths_s[r] for r in range(reqs)]
    beyond = [
        length[r] - PAGE * sum((t >= 0).astype(I32) for t in table[r]) for r in range(reqs)
    ]
    shape = (reqs, 128)
    borrow = [column([borrowed_s[j, r] for r in range(reqs)], shape) for j in range(RANKS)]
    left = column(beyond, shape)
    counted = [jnp.clip(left - PAGE * j, 0, PAGE).astype(F32) for j in range(RANKS)]
    lane = lax.broadcasted_iota(I32, shape, 1)
    total_slots = n_inst * slots
    wanted, counts = [], []
    for base in range(0, total_slots, 128):
        block = (lane + base) // slots
        other, place = block // n_chip, block % n_chip
        dy = jnp.where(place < half - 1, place + 1, place + 2)
        dy = jnp.where(place < n_near, dy, jnp.where(place == n_near, half, 0))
        name = chip_at(dy, other) * slots + lane % slots
        wanted.append(((borrow[0] == name) | (borrow[1] == name)).astype(F32))
        hit = [b == lane + base for b in borrow]
        both = jnp.where(hit[0], counted[0], 0.0) + jnp.where(hit[1], counted[1], 0.0)
        counts.append(jnp.sum(both, axis=0, keepdims=True))
    wanted = jnp.concatenate(wanted, axis=1)[:, :total_slots].astype(BF16)
    counts = jnp.concatenate(counts, axis=1)
    q = q_v[...]
    asked = dot(wanted, q, ((0,), (0,))).astype(BF16)
    ask_out[...] = asked.reshape(n_inst, slots, 2 * HD)
    count_out[...] = counts
    ask_in[n_near + 3] = ask_out[n_near + 1]

    pl.semaphore_wait(barrier, greeted)

    def send(src, dst, phase, to):
        pltpu.make_async_remote_copy(
            src_ref=src, dst_ref=dst, send_sem=send_sem.at[phase], recv_sem=recv_sem.at[phase], device_id=to
        ).start()

    def to_chips(chips, act):
        for y in chips:

            @pl.when(y != me // 2)
            def _():
                act(2 * y + 1 - me % 2)
                act(2 * y + me % 2)

        act(me + 1 - 2 * (me % 2))

    def arrive(ref, count, phase):
        part = ref.at[pl.ds(0, count)]
        pltpu.make_async_copy(part, part, recv_sem.at[phase]).wait()

    def sent(ref, count, phase):
        part = ref.at[pl.ds(0, count)]
        pltpu.make_async_copy(part, part, send_sem.at[phase]).wait()

    over = {"inst": sibling}
    for other in range(2):
        to = {"inst": chip_at(half, other)}
        send(ask_out.at[other * n_chip + n_near], ask_in.at[n_near + other], 0, to)
        send(count_out, count_in.at[n_near + other], 1, to)
    send(ask_out.at[pl.ds(n_chip, n_near)], ask_relay, 5, over)
    send(count_out, count_relay, 6, over)
    send(ask_out.at[n_chip + n_near + 1], ask_in.at[n_near + 2], 0, over)
    arrive(ask_relay, n_near, 5)
    arrive(count_relay, 1, 6)
    for p in range(n_near):
        ask_out[p] = ask_out[p] + ask_relay[p]
    count_sum[...] = counts + count_relay[...]
    for p in far_first:
        to = {"inst": chip_at(near[p])}
        send(ask_out.at[p], ask_in.at[p], 0, to)
        send(count_sum, count_in.at[p], 1, to)
    tell(0)

    row = lax.broadcasted_iota(I32, (2 * reqs, PAGE), 0) % reqs
    token = lax.broadcasted_iota(I32, (2 * reqs, PAGE), 1)
    q2 = by_head(q)
    loads[4].wait()
    scores = [jnp.zeros((2 * reqs, PAGE), F32) for _ in range(RANKS)]
    usable = [jnp.zeros((2 * reqs, PAGE), I32) for _ in range(RANKS)]
    for r in range(reqs):
        for j in range(RANKS):
            page = jnp.maximum(table[r][j], 0)
            s = dot(q2, home_v[page, 0, :, :HD], ((1,), (1,)))
            scores[j] = jnp.where(row == r, s, scores[j])
            here = jnp.where(table[r][j] >= 0, length[r] - PAGE * j, 0)
            usable[j] = jnp.where(row == r, here, usable[j])
    usable = [token < u for u in usable]
    scores = [jnp.where(u, s * scale, SENTINEL) for u, s in zip(usable, scores)]
    home_max = jnp.max(jnp.maximum(scores[0], scores[1]), axis=1, keepdims=True)
    home_w = [
        jnp.where(u, jnp.exp(s - home_max), 0.0).astype(BF16) for u, s in zip(usable, scores)
    ]
    home_total = sum(jnp.sum(w.astype(F32), axis=1, keepdims=True) for w in home_w)
    home_sum = jnp.zeros((2 * reqs, HD), F32)
    for r in range(reqs):
        o = 0.0
        for j in range(RANKS):
            page = jnp.maximum(table[r][j], 0)
            o = o + dot(home_w[j], home_v[page, 0, :, HD:])
        home_sum = jnp.where(row == r, o, home_sum)

    told(0)
    tell(1)

    loads[5].wait()
    for p in range(slots):
        keys_v[p * HD : (p + 1) * HD] = lent_v[p, 0, :, :HD].T
    lrow = lax.broadcasted_iota(I32, (2 * slots, PAGE), 0)
    llane = lax.broadcasted_iota(I32, (2 * slots, PAGE), 1)
    own = [(lrow % slots == p).astype(F32).astype(BF16) for p in range(slots)]

    def spread(x):
        return jnp.concatenate([x * o for o in own], axis=1)

    arrive(ask_in, n_near + 3, 0)
    arrive(count_in, n_near + 2, 1)
    q_lent = ask_in[0]
    for k in range(1, n_near + 4):
        q_lent = q_lent + ask_in[k]
    q_lent = by_head(q_lent)
    count_row = jnp.sum(count_in[...], axis=0) + counts + count_relay[...]
    wide = (slots, count_row.shape[1])
    mine = lax.broadcasted_iota(I32, wide, 1) == me * slots + lax.broadcasted_iota(I32, wide, 0)
    count_col = jnp.sum(jnp.where(mine, count_row, 0.0), axis=1, keepdims=True)
    count_col = jnp.concatenate([count_col, count_col], axis=0)
    s = dot(spread(q_lent), keys_v[...])
    ok = llane < count_col.astype(I32)
    s = jnp.where(ok, s * scale, SENTINEL)
    lent_max = jnp.max(s, axis=1, keepdims=True)
    w = jnp.where(ok, jnp.exp(s - lent_max), 0.0).astype(BF16)
    lent_total = jnp.sum(w.astype(F32), axis=1, keepdims=True)
    o = dot(spread(w), lent_v[:, 0, :, HD:].reshape(slots * PAGE, HD))
    part = by_lane(o).astype(BF16)
    stats = jnp.where(llane == lrow, lent_max, 0.0) + jnp.where(
        llane == lrow + 2 * slots, lent_total, 0.0
    )
    stats = jnp.sum(stats, axis=0, keepdims=True)
    part_out[...] = part
    stat_out[...] = stats
    part_in[n_inst - 1] = part
    stat_in[n_inst - 1] = stats
    def answer(to):
        place = (to - me - 1) % n_inst
        send(stat_out, stat_in.at[place], 3, {"inst": to})
        send(part_out, part_in.at[place], 2, {"inst": to})

    to_chips(sorted(range(n_chip), key=lambda y: min(y, n_chip + 1 - y)), answer)

    told(1)
    tell(2)

    two = jnp.concatenate(borrow, axis=0)
    gather = []
    for base in range(0, total_slots, 128):
        i = base + lax.broadcasted_iota(I32, two.shape, 1)
        name = (me - i // slots - 1) % n_inst * slots + i % slots
        gather.append((two == name).astype(F32))
    gather = jnp.concatenate(gather, axis=1)[:, :total_slots].astype(BF16)
    lane2 = lax.broadcasted_iota(I32, two.shape, 1)
    lender = ((me - lane2 - 1) % n_inst == two // slots) & (lane2 < n_inst) & (two >= 0)
    lender = lender[:, :n_inst].astype(F32).astype(BF16)
    slot = jnp.where(two >= 0, two % slots, -1)

    arrive(stat_in, n_inst - 1, 3)
    left_over = stat_in[...].reshape(n_inst, 128)
    pieces = []
    for _ in range(3):
        pieces.append(left_over.astype(BF16))
        left_over = left_over - pieces[-1].astype(F32)
    found = dot(jnp.concatenate([lender] * 3, axis=1), jnp.concatenate(pieces, axis=0))
    present = two[:, :1] >= 0

    def pick(kind, absent):
        value = jnp.sum(jnp.where(lane2 == slot + kind * slots, found, 0.0), axis=1, keepdims=True)
        value = jnp.where((slot[:, :1] >= 0), value, absent)
        return [value[j * reqs : (j + 1) * reqs] for j in range(RANKS)]

    max0, max1 = pick(0, SENTINEL), pick(1, SENTINEL)
    tot0, tot1 = pick(2, 0.0), pick(3, 0.0)
    page_max = [jnp.concatenate([max0[j], max1[j]], axis=0) for j in range(RANKS)]
    page_total = [jnp.concatenate([tot0[j], tot1[j]], axis=0) for j in range(RANKS)]
    summit = jnp.maximum(home_max, jnp.maximum(page_max[0], page_max[1]))
    home_share = jnp.exp(home_max - summit)
    share = [jnp.exp(m - summit) for m in page_max]
    total = home_share * home_total + share[0] * page_total[0] + share[1] * page_total[1]
    total = jnp.maximum(total, 1.0)
    arrive(part_in, n_inst - 1, 2)
    got = dot(gather, part_in[...].reshape(total_slots, 2 * HD))
    attended = home_share * home_sum
    for j in range(RANKS):
        attended = attended + share[j] * by_head(got[j * reqs : (j + 1) * reqs])
    attended = by_lane(attended / total).astype(BF16)

    loads[6].wait()
    told(2)
    def project(z):
        start = pl.multiple_of(z * (nx * 128), nx * 128)
        block = dot(attended, weight_v[:, pl.ds(start, nx * 128)]).astype(BF16)
        for x in range(nx):
            proj_out[z * nx + x] = block[:, x * 128 : (x + 1) * 128]

    def hand_over(z, x):
        place = (z - my_z) % nz * nx + (x - my_x) % nx - 1
        send(proj_out.at[z * nx + x], proj_in.at[place], 4, {"tp": z * nx + x})

    for z in range(nz):
        project(z)

        @pl.when(z != my_z)
        def _():
            for x in range(nx):
                hand_over(z, x)

    for d in range(1, nx):
        hand_over(my_z, (my_x + d) % nx)
    sent(ask_in, n_near + 3, 0)
    sent(count_in, n_near + 2, 1)
    sent(ask_relay, n_near, 5)
    sent(count_relay, 1, 6)
    sent(part_in, n_inst - 1, 2)
    sent(stat_in, n_inst - 1, 3)
    sent(proj_in, n_tp - 1, 4)
    arrive(proj_in, n_tp - 1, 4)
    terms = [proj_out[tp].astype(F32)] + [proj_in[k].astype(F32) for k in range(n_tp - 1)]
    while len(terms) > 1:
        terms = [sum(terms[k : k + 2]) for k in range(0, len(terms), 2)]
    out_ref[...] = terms[0].astype(out_ref.dtype)


def shards(nx, queries, home_kv, lent_kv, page_table, borrowed, lengths, out_weight):
    n_inst, n_tp = lax.axis_size("inst"), lax.axis_size("tp")
    reqs = queries.shape[0]
    slots = lent_kv.shape[0]
    cols = out_weight.shape[1] // n_tp
    lanes = -(-n_inst * slots // 128) * 128
    return pl.pallas_call(
        functools.partial(fused, n_inst, n_tp // nx, nx),
        out_shape=jax.ShapeDtypeStruct((reqs, cols), BF16),
        in_specs=[pl.BlockSpec(memory_space=pltpu.HBM)] * 7,
        out_specs=pl.BlockSpec(memory_space=pltpu.VMEM),
        scratch_shapes=[
            pltpu.VMEM(queries.shape, BF16),
            pltpu.VMEM(home_kv.shape, BF16),
            pltpu.VMEM(lent_kv.shape, BF16),
            pltpu.VMEM(out_weight.shape, BF16),
            pltpu.SMEM(page_table.shape[::-1], I32),
            pltpu.SMEM(borrowed.shape[::-1], I32),
            pltpu.SMEM(lengths.shape, I32),
            pltpu.VMEM((n_inst, slots, 2 * HD), BF16),
            pltpu.VMEM((n_inst // 2 + 2, slots, 2 * HD), BF16),
            pltpu.VMEM((n_inst // 2 - 2, slots, 2 * HD), BF16),
            pltpu.VMEM((1, lanes), F32),
            pltpu.VMEM((n_inst // 2, 1, lanes), F32),
            pltpu.VMEM((1, lanes), F32),
            pltpu.VMEM((1, lanes), F32),
            pltpu.VMEM((slots, 2 * HD), BF16),
            pltpu.VMEM((n_inst, slots, 2 * HD), BF16),
            pltpu.VMEM((1, 128), F32),
            pltpu.VMEM((n_inst, 1, 128), F32),
            pltpu.VMEM((n_tp, reqs, cols), BF16),
            pltpu.VMEM((n_tp - 1, reqs, cols), BF16),
            pltpu.VMEM((slots * HD, PAGE), BF16),
            pltpu.SemaphoreType.DMA((7,)),
            pltpu.SemaphoreType.DMA((7,)),
            pltpu.SemaphoreType.DMA((7,)),
            pltpu.SemaphoreType.REGULAR((3,)),
        ],
        compiler_params=pltpu.CompilerParams(
            collective_id=0, has_side_effects=True, vmem_limit_bytes=40 * 1024 * 1024
        ),
    )(*[pltpu.with_memory_space_constraint(x, pltpu.HBM) for x in (queries, home_kv, lent_kv, page_table.T, borrowed.T, lengths, out_weight)])


def solution(mesh):
    n_tp = mesh.shape["tp"]
    nx = 4 if n_tp % 4 == 0 else 1
    placed = (
        P("inst", "tp"),
        P("inst", "tp", None, None),
        P("inst", "tp", None, None),
        P("inst", None),
        P("inst", None),
        P("inst"),
        P("tp", None),
    )
    return jax.shard_map(
        functools.partial(shards, nx), mesh=mesh, in_specs=placed, out_specs=P("inst", "tp"), check_vma=False
    )
```

```python
import functools
import math

import jax
import jax.numpy as jnp
from jax import lax
from jax.experimental import pallas as pl
from jax.experimental.pallas import tpu as pltpu
from jax.sharding import PartitionSpec as P

HD = 128
PAGE = 128
RANKS = 2
SENTINEL = -1e30
F32 = jnp.float32
BF16 = jnp.bfloat16
I32 = jnp.int32


def column(values, shape):
    row = lax.broadcasted_iota(I32, shape, 0)
    out = jnp.full(shape, values[0], I32)
    for r in range(1, len(values)):
        out = jnp.where(row == r, values[r], out)
    return out


def dot(a, b, dims=((1,), (0,))):
    return lax.dot_general(a, b, (dims, ((), ())), preferred_element_type=F32)


def by_head(x):
    return jnp.concatenate([x[:, :HD], x[:, HD:]], axis=0)


def by_lane(x):
    rows = x.shape[0] // 2
    return jnp.concatenate([x[:rows], x[rows:]], axis=1)


def fused(
    n_inst, nz, nx,
    q_hbm, home_hbm, lent_hbm, table_hbm, borrowed_hbm, lengths_hbm, weight_hbm,
    out_ref,
    q_v, home_v, lent_v, weight_v, table_s, borrowed_s, lengths_s,
    ask_out, ask_in, ask_relay, count_out, count_in, count_relay, count_sum, part_out, part_in, stat_out, stat_in, proj_out, proj_in,
    keys_v, load_sem, send_sem, recv_sem, here_sem,
):
    n_tp = nz * nx
    slots = lent_v.shape[0]
    reqs = q_v.shape[0]
    me = lax.axis_index("inst")
    tp = lax.axis_index("tp")
    my_z, my_x = tp // nx, tp % nx
    my_y, my_c = me // 2, me % 2
    n_chip = n_inst // 2
    half = n_chip // 2
    near = [d for d in range(1, n_chip) if d != half]
    n_near = len(near)
    far_first = sorted(range(n_near), key=lambda p: -min(near[p], n_chip - near[p]))
    sibling = me + 1 - 2 * my_c

    def chip_at(dy, other=0):
        return (my_y + dy) % n_chip * 2 + (my_c + other - 2 * my_c * other)
    scale = 1.0 / math.sqrt(HD)

    barrier = pltpu.get_barrier_semaphore()
    order = sorted(range(1, n_inst), key=lambda k: -min(k, n_inst - k))
    rounds = []
    step = 1
    while step <= nz // 2:
        rounds.append(sorted({step, nz - step}))
        step *= 2

    def along_z(d):
        return {"tp": (my_z + d) % nz * nx + my_x}

    for k in order:
        pl.semaphore_signal(barrier, 1, device_id={"inst": (me + k) % n_inst})
    for d in range(1, nx):
        pl.semaphore_signal(barrier, 1, device_id={"tp": my_z * nx + (my_x + d) % nx})
    for d in rounds[0] if rounds else []:
        pl.semaphore_signal(barrier, 1, device_id=along_z(d))
    greeted = n_inst - 1 + nx - 1 + (len(rounds[0]) if rounds else 0)

    def tell(i):
        for d in rounds[i] if i < len(rounds) else []:
            pl.semaphore_signal(here_sem.at[i], 1, device_id=along_z(d))

    def told(i):
        if i < len(rounds):
            pl.semaphore_wait(here_sem.at[i], len(rounds[i]))

    loads = []
    for i, (src, dst) in enumerate(
        [
            (table_hbm, table_s),
            (borrowed_hbm, borrowed_s),
            (lengths_hbm, lengths_s),
            (q_hbm, q_v),
            (home_hbm, home_v),
            (lent_hbm, lent_v),
            (weight_hbm, weight_v),
        ]
    ):
        copy = pltpu.make_async_copy(src, dst, load_sem.at[i])
        copy.start()
        loads.append(copy)

    for copy in loads[:4]:
        copy.wait()

    table = [[table_s[j, r] for j in range(RANKS)] for r in range(reqs)]
    length = [lengths_s[r] for r in range(reqs)]
    beyond = [
        length[r] - PAGE * sum((t >= 0).astype(I32) for t in table[r]) for r in range(reqs)
    ]
    shape = (reqs, 128)
    borrow = [column([borrowed_s[j, r] for r in range(reqs)], shape) for j in range(RANKS)]
    left = column(beyond, shape)
    counted = [jnp.clip(left - PAGE * j, 0, PAGE).astype(F32) for j in range(RANKS)]
    lane = lax.broadcasted_iota(I32, shape, 1)
    total_slots = n_inst * slots
    wanted, counts = [], []
    for base in range(0, total_slots, 128):
        block = (lane + base) // slots
        other, place = block // n_chip, block % n_chip
        dy = jnp.where(place < half - 1, place + 1, place + 2)
        dy = jnp.where(place < n_near, dy, jnp.where(place == n_near, half, 0))
        name = chip_at(dy, other) * slots + lane % slots
        wanted.append(((borrow[0] == name) | (borrow[1] == name)).astype(F32))
        hit = [b == lane + base for b in borrow]
        both = jnp.where(hit[0], counted[0], 0.0) + jnp.where(hit[1], counted[1], 0.0)
        counts.append(jnp.sum(both, axis=0, keepdims=True))
    wanted = jnp.concatenate(wanted, axis=1)[:, :total_slots].astype(BF16)
    counts = jnp.concatenate(counts, axis=1)
    q = q_v[...]
    asked = dot(wanted, q, ((0,), (0,))).astype(BF16)
    ask_out[...] = asked.reshape(n_inst, slots, 2 * HD)
    count_out[...] = counts
    ask_in[n_near + 3] = ask_out[n_near + 1]

    pl.semaphore_wait(barrier, greeted)

    def send(src, dst, phase, to):
        pltpu.make_async_remote_copy(
            src_ref=src, dst_ref=dst, send_sem=send_sem.at[phase], recv_sem=recv_sem.at[phase], device_id=to
        ).start()

    def to_chips(chips, act):
        for y in chips:

            @pl.when(y != me // 2)
            def _():
                act(2 * y + 1 - me % 2)
                act(2 * y + me % 2)

        act(me + 1 - 2 * (me % 2))

    def arrive(ref, count, phase):
        part = ref.at[pl.ds(0, count)]
        pltpu.make_async_copy(part, part, recv_sem.at[phase]).wait()

    def sent(ref, count, phase):
        part = ref.at[pl.ds(0, count)]
        pltpu.make_async_copy(part, part, send_sem.at[phase]).wait()

    over = {"inst": sibling}
    for other in range(2):
        to = {"inst": chip_at(half, other)}
        send(ask_out.at[other * n_chip + n_near], ask_in.at[n_near + other], 0, to)
        send(count_out, count_in.at[n_near + other], 1, to)
    send(ask_out.at[pl.ds(n_chip, n_near)], ask_relay, 5, over)
    send(count_out, count_relay, 6, over)
    send(ask_out.at[n_chip + n_near + 1], ask_in.at[n_near + 2], 0, over)
    arrive(ask_relay, n_near, 5)
    arrive(count_relay, 1, 6)
    for p in range(n_near):
        ask_out[p] = ask_out[p] + ask_relay[p]
    count_sum[...] = counts + count_relay[...]
    for p in far_first:
        to = {"inst": chip_at(near[p])}
        send(ask_out.at[p], ask_in.at[p], 0, to)
        send(count_sum, count_in.at[p], 1, to)
    tell(0)

    told(0)
    tell(1)

    loads[5].wait()
    for p in range(slots):
        keys_v[p * HD : (p + 1) * HD] = lent_v[p, 0, :, :HD].T
    lrow = lax.broadcasted_iota(I32, (2 * slots, PAGE), 0)
    llane = lax.broadcasted_iota(I32, (2 * slots, PAGE), 1)
    own = [(lrow % slots == p).astype(F32).astype(BF16) for p in range(slots)]

    def spread(x):
        return jnp.concatenate([x * o for o in own], axis=1)

    arrive(ask_in, n_near + 3, 0)
    arrive(count_in, n_near + 2, 1)
    q_lent = ask_in[0]
    for k in range(1, n_near + 4):
        q_lent = q_lent + ask_in[k]
    q_lent = by_head(q_lent)
    count_row = jnp.sum(count_in[...], axis=0) + counts + count_relay[...]
    wide = (slots, count_row.shape[1])
    mine = lax.broadcasted_iota(I32, wide, 1) == me * slots + lax.broadcasted_iota(I32, wide, 0)
    count_col = jnp.sum(jnp.where(mine, count_row, 0.0), axis=1, keepdims=True)
    count_col = jnp.concatenate([count_col, count_col], axis=0)
    s = dot(spread(q_lent), keys_v[...])
    ok = llane < count_col.astype(I32)
    s = jnp.where(ok, s * scale, SENTINEL)
    lent_max = jnp.max(s, axis=1, keepdims=True)
    w = jnp.where(ok, jnp.exp(s - lent_max), 0.0).astype(BF16)
    lent_total = jnp.sum(w.astype(F32), axis=1, keepdims=True)
    o = dot(spread(w), lent_v[:, 0, :, HD:].reshape(slots * PAGE, HD))
    part = by_lane(o).astype(BF16)
    stats = jnp.where(llane == lrow, lent_max, 0.0) + jnp.where(
        llane == lrow + 2 * slots, lent_total, 0.0
    )
    stats = jnp.sum(stats, axis=0, keepdims=True)
    part_out[...] = part
    stat_out[...] = stats
    part_in[n_inst - 1] = part
    stat_in[n_inst - 1] = stats
    def answer(to):
        place = (to - me - 1) % n_inst
        send(stat_out, stat_in.at[place], 3, {"inst": to})
        send(part_out, part_in.at[place], 2, {"inst": to})

    to_chips(sorted(range(n_chip), key=lambda y: min(y, n_chip + 1 - y)), answer)

    told(1)
    tell(2)

    row = lax.broadcasted_iota(I32, (2 * reqs, PAGE), 0) % reqs
    token = lax.broadcasted_iota(I32, (2 * reqs, PAGE), 1)
    q2 = by_head(q)
    loads[4].wait()
    scores = [jnp.zeros((2 * reqs, PAGE), F32) for _ in range(RANKS)]
    usable = [jnp.zeros((2 * reqs, PAGE), I32) for _ in range(RANKS)]
    for r in range(reqs):
        for j in range(RANKS):
            page = jnp.maximum(table[r][j], 0)
            s = dot(q2, home_v[page, 0, :, :HD], ((1,), (1,)))
            scores[j] = jnp.where(row == r, s, scores[j])
            here = jnp.where(table[r][j] >= 0, length[r] - PAGE * j, 0)
            usable[j] = jnp.where(row == r, here, usable[j])
    usable = [token < u for u in usable]
    scores = [jnp.where(u, s * scale, SENTINEL) for u, s in zip(usable, scores)]
    home_max = jnp.max(jnp.maximum(scores[0], scores[1]), axis=1, keepdims=True)
    home_w = [
        jnp.where(u, jnp.exp(s - home_max), 0.0).astype(BF16) for u, s in zip(usable, scores)
    ]
    home_total = sum(jnp.sum(w.astype(F32), axis=1, keepdims=True) for w in home_w)
    home_sum = jnp.zeros((2 * reqs, HD), F32)
    for r in range(reqs):
        o = 0.0
        for j in range(RANKS):
            page = jnp.maximum(table[r][j], 0)
            o = o + dot(home_w[j], home_v[page, 0, :, HD:])
        home_sum = jnp.where(row == r, o, home_sum)

    two = jnp.concatenate(borrow, axis=0)
    gather = []
    for base in range(0, total_slots, 128):
        i = base + lax.broadcasted_iota(I32, two.shape, 1)
        name = (me - i // slots - 1) % n_inst * slots + i % slots
        gather.append((two == name).astype(F32))
    gather = jnp.concatenate(gather, axis=1)[:, :total_slots].astype(BF16)
    lane2 = lax.broadcasted_iota(I32, two.shape, 1)
    lender = ((me - lane2 - 1) % n_inst == two // slots) & (lane2 < n_inst) & (two >= 0)
    lender = lender[:, :n_inst].astype(F32).astype(BF16)
    slot = jnp.where(two >= 0, two % slots, -1)

    arrive(stat_in, n_inst - 1, 3)
    left_over = stat_in[...].reshape(n_inst, 128)
    pieces = []
    for _ in range(3):
        pieces.append(left_over.astype(BF16))
        left_over = left_over - pieces[-1].astype(F32)
    found = dot(jnp.concatenate([lender] * 3, axis=1), jnp.concatenate(pieces, axis=0))
    present = two[:, :1] >= 0

    def pick(kind, absent):
        value = jnp.sum(jnp.where(lane2 == slot + kind * slots, found, 0.0), axis=1, keepdims=True)
        value = jnp.where((slot[:, :1] >= 0), value, absent)
        return [value[j * reqs : (j + 1) * reqs] for j in range(RANKS)]

    max0, max1 = pick(0, SENTINEL), pick(1, SENTINEL)
    tot0, tot1 = pick(2, 0.0), pick(3, 0.0)
    page_max = [jnp.concatenate([max0[j], max1[j]], axis=0) for j in range(RANKS)]
    page_total = [jnp.concatenate([tot0[j], tot1[j]], axis=0) for j in range(RANKS)]
    summit = jnp.maximum(home_max, jnp.maximum(page_max[0], page_max[1]))
    home_share = jnp.exp(home_max - summit)
    share = [jnp.exp(m - summit) for m in page_max]
    total = home_share * home_total + share[0] * page_total[0] + share[1] * page_total[1]
    total = jnp.maximum(total, 1.0)
    arrive(part_in, n_inst - 1, 2)
    got = dot(gather, part_in[...].reshape(total_slots, 2 * HD))
    attended = home_share * home_sum
    for j in range(RANKS):
        attended = attended + share[j] * by_head(got[j * reqs : (j + 1) * reqs])
    attended = by_lane(attended / total).astype(BF16)

    loads[6].wait()
    told(2)
    def project(z):
        start = pl.multiple_of(z * (nx * 128), nx * 128)
        block = dot(attended, weight_v[:, pl.ds(start, nx * 128)]).astype(BF16)
        for x in range(nx):
            proj_out[z * nx + x] = block[:, x * 128 : (x + 1) * 128]

    def hand_over(z, x):
        place = (z - my_z) % nz * nx + (x - my_x) % nx - 1
        send(proj_out.at[z * nx + x], proj_in.at[place], 4, {"tp": z * nx + x})

    for z in range(nz):
        project(z)

        @pl.when(z != my_z)
        def _():
            for x in range(nx):
                hand_over(z, x)

    for d in range(1, nx):
        hand_over(my_z, (my_x + d) % nx)
    sent(ask_in, n_near + 3, 0)
    sent(count_in, n_near + 2, 1)
    sent(ask_relay, n_near, 5)
    sent(count_relay, 1, 6)
    sent(part_in, n_inst - 1, 2)
    sent(stat_in, n_inst - 1, 3)
    sent(proj_in, n_tp - 1, 4)
    arrive(proj_in, n_tp - 1, 4)
    terms = [proj_out[tp].astype(F32)] + [proj_in[k].astype(F32) for k in range(n_tp - 1)]
    while len(terms) > 1:
        terms = [sum(terms[k : k + 2]) for k in range(0, len(terms), 2)]
    out_ref[...] = terms[0].astype(out_ref.dtype)


def shards(nx, queries, home_kv, lent_kv, page_table, borrowed, lengths, out_weight):
    n_inst, n_tp = lax.axis_size("inst"), lax.axis_size("tp")
    reqs = queries.shape[0]
    slots = lent_kv.shape[0]
    cols = out_weight.shape[1] // n_tp
    lanes = -(-n_inst * slots // 128) * 128
    return pl.pallas_call(
        functools.partial(fused, n_inst, n_tp // nx, nx),
        out_shape=jax.ShapeDtypeStruct((reqs, cols), BF16),
        in_specs=[pl.BlockSpec(memory_space=pltpu.HBM)] * 7,
        out_specs=pl.BlockSpec(memory_space=pltpu.VMEM),
        scratch_shapes=[
            pltpu.VMEM(queries.shape, BF16),
            pltpu.VMEM(home_kv.shape, BF16),
            pltpu.VMEM(lent_kv.shape, BF16),
            pltpu.VMEM(out_weight.shape, BF16),
            pltpu.SMEM(page_table.shape[::-1], I32),
            pltpu.SMEM(borrowed.shape[::-1], I32),
            pltpu.SMEM(lengths.shape, I32),
            pltpu.VMEM((n_inst, slots, 2 * HD), BF16),
            pltpu.VMEM((n_inst // 2 + 2, slots, 2 * HD), BF16),
            pltpu.VMEM((n_inst // 2 - 2, slots, 2 * HD), BF16),
            pltpu.VMEM((1, lanes), F32),
            pltpu.VMEM((n_inst // 2, 1, lanes), F32),
            pltpu.VMEM((1, lanes), F32),
            pltpu.VMEM((1, lanes), F32),
            pltpu.VMEM((slots, 2 * HD), BF16),
            pltpu.VMEM((n_inst, slots, 2 * HD), BF16),
            pltpu.VMEM((1, 128), F32),
            pltpu.VMEM((n_inst, 1, 128), F32),
            pltpu.VMEM((n_tp, reqs, cols), BF16),
            pltpu.VMEM((n_tp - 1, reqs, cols), BF16),
            pltpu.VMEM((slots * HD, PAGE), BF16),
            pltpu.SemaphoreType.DMA((7,)),
            pltpu.SemaphoreType.DMA((7,)),
            pltpu.SemaphoreType.DMA((7,)),
            pltpu.SemaphoreType.REGULAR((3,)),
        ],
        compiler_params=pltpu.CompilerParams(
            collective_id=0, has_side_effects=True, vmem_limit_bytes=40 * 1024 * 1024
        ),
    )(*[pltpu.with_memory_space_constraint(x, pltpu.HBM) for x in (queries, home_kv, lent_kv, page_table.T, borrowed.T, lengths, out_weight)])


def solution(mesh):
    n_tp = mesh.shape["tp"]
    nx = 4 if n_tp % 4 == 0 else 1
    placed = (
        P("inst", "tp"),
        P("inst", "tp", None, None),
        P("inst", "tp", None, None),
        P("inst", None),
        P("inst", None),
        P("inst"),
        P("tp", None),
    )
    return jax.shard_map(
        functools.partial(shards, nx), mesh=mesh, in_specs=placed, out_specs=P("inst", "tp"), check_vma=False
    )
```
